256 devices in a mesh: shell: 8 (over x, core), radial: 32 (over z, y).
Axes of the slice: x: 4, y: 4, z: 8, core: 2. Of those that a mesh axis runs over, the one named last changes fastest.
Arguments:
- density: float32 [32, 128, 4096], P('radial', 'shell'), may hold values from -6 to 6
- footprint: int32 [32, 128, 4096], P('radial', 'shell'), may hold values 0 or 1
- cycle_index: int32 [128], P('shell'), may hold values from 2944 to 3071, as said below
- order_values: int32 [64], replicated, may hold values from 0 to 2047, as said below
- block_lengths: int32 [32], replicated, may hold values from 1 to 128, 2048 in all
- legendre: bfloat16 [64, 2048, 128], P('shell'), may hold values from -0.0078125 to 0.0078125
- bessel: bfloat16 [32, 2048, 512], P('radial', None, 'shell'), may hold values from -2 to 2
Outputs:
- sfb: bfloat16 [4096, 512, 128], P('radial', 'shell')
The draws below stay inside these ranges and needn't reach their ends.
Inputs may be any that keep to these rules, and one draw needn't show every extreme that they name: `order_values`: 64 different orders, 0 and 2047 among them. `cycle_index`: 128 different row numbers forming the contiguous band that ends at row 3071, in any order over the slots.
All inputs are finite; a program needn't handle non-finite values. No bound on the sum of `footprint` on one device may be relied on, other than what follows from the above.
Results may differ from the reference program's by a relative error of at most 0.0049.
The reference program's roundings to bfloat16 on the way (of `four` and `harmonic`) count: a program that leaves them out, or rounds other values in their place, can miss the bound.
Values may be sent and summed in bfloat16 or wider, within the bound.
No kernel may reach another device: no remote copies, remote signals or barrier semaphores. Data moves between devices by JAX's collectives and lax.ppermute only.
A program may use at most 64 MiB of HBM per device.

```python
import math
import jax
import jax.numpy as jnp
import numpy as np
from jax import lax

NSIDE = 1024
NPHI = 4096
DEG = 2048
NMODES = 512
SHELLS = 32
CYCLES = 128
ORDERS = 64
BLOCK_CAP = 128
SLOTS = 4096
N_RADIAL = 32


def draw_cycle_index(key, part):
    key = jax.random.fold_in(key, 7)
    order = jax.random.permutation(jax.random.fold_in(key, 2), CYCLES)
    return (3 * NSIDE - CYCLES + order).astype(jnp.int32)


def draw_order_values(key, part):
    key = jax.random.fold_in(key, 11)
    inner = jax.random.permutation(jax.random.fold_in(key, 1), DEG - 2)[:ORDERS - 2] + 1
    values = jnp.concatenate([jnp.array([0, DEG - 1], jnp.int32), inner.astype(jnp.int32)])
    mixing = jax.random.permutation(jax.random.fold_in(key, 2), ORDERS)
    return values[mixing].astype(jnp.int32)


def set_ends(values, own_key, low, largest):
    longest = values.shape.index(max(values.shape))
    spots = []
    for shift in (0, 1):
        where = [jax.random.randint(jax.random.fold_in(own_key, axis), (), 0, length) for axis, length in enumerate(values.shape)]
        where[longest] = (where[longest] + shift) % values.shape[longest]
        spots.append(tuple(where))
    return values.at[spots[0]].set(low).at[spots[1]].set(largest)


def spiked(entries, key, source, target, parts, factor):
    def block_of(position):
        return (jnp.arange(entries.shape[position]) // (entries.shape[position] // parts)).reshape((-1,) + (1,) * (entries.ndim - 1 - position))

    first = jax.random.permutation(key, parts)[block_of(target)]
    second = (block_of(target) + parts // 2) % parts
    return jnp.where((block_of(source) == first) | (block_of(source) == second), factor * entries, entries)


def block_scale(own_key, shape, pieces, least, top_value):
    factor_of, own = 1.0, jax.random.fold_in(own_key, 6)
    for position, shards_of in pieces:
        steps = jnp.exp(jax.random.uniform(jax.random.fold_in(own, position), (shards_of,), jnp.float32, least / len(pieces), top_value / len(pieces)))
        factor_of = factor_of * jnp.repeat(steps, shape[position] // shards_of).reshape([-1 if axis == position else 1 for axis in range(len(shape))])
    return factor_of


def profile(amount, total, limit, skew):
    weights = [(1 << 20) // math.isqrt(grade ** skew) + 1 for grade in range(2, amount + 1)]
    rest, given = total - limit - (amount - 1), [1] * (amount - 1)
    while rest > 0:
        movable = [i for i in range(amount - 1) if given[i] < limit]
        mass, left = sum([weights[i] for i in movable]), rest
        for i in movable:
            addition = min(limit - given[i], max(1, left * weights[i] // mass), rest)
            given[i] = given[i] + addition
            rest = rest - addition
    return np.array([limit] + given)


def uneven(rng, count, total, most, lean):
    if count == 2:
        one = jax.random.randint(rng, (), max(1, total - most), min(most, total - 1) + 1)
        return jnp.stack([one, total - one])
    sizes = jnp.asarray(profile(count, total, most, lean), jnp.int32)
    twos = (count - 1) // 2
    giver, sink = sizes[1:1 + 2 * twos:2], sizes[2:2 + 2 * twos:2]
    margin = jnp.minimum(giver - 1, most - sink)
    shifted = jax.random.randint(jax.random.fold_in(rng, 1), (twos,), 0, 1 << 20) % (margin + 1)
    sizes = sizes.at[1:1 + 2 * twos:2].set(giver - shifted).at[2:2 + 2 * twos:2].set(sink + shifted)
    return sizes[jax.random.permutation(jax.random.fold_in(rng, 2), count)]


def gaussian(key, shape, width, limit, cuts=(), kind=jnp.bfloat16):
    values = width * jax.random.normal(key, shape, jnp.float32)
    if cuts:
        values = values * block_scale(key, shape, cuts, -0.22, 0.18)
    return jnp.clip(values, -limit, limit).astype(kind)


def bell_draw_with(key, extent, deviation, most, split, heavy, dtype=jnp.bfloat16):
    values = deviation * jax.random.normal(key, extent, jnp.float32)
    if split:
        values = values * block_scale(key, extent, split, -0.22, 0.18)
    return jnp.clip(spiked(values, jax.random.fold_in(key, 3), *heavy), -most, most).astype(dtype)


def setup_inputs(seed: int = 0) -> dict:
    arg_keys = jax.random.split(jax.random.key(seed), 8)
    density = gaussian(arg_keys[0], (SHELLS, CYCLES, NPHI), 1.0, 6.0, ((0, 32), (1, 8)), jnp.float32)
    footprint = set_ends((jax.random.randint(arg_keys[1], (SHELLS, CYCLES, NPHI), 0, 4) < 3).astype(jnp.int32), jax.random.fold_in(arg_keys[1], 1), 0, 1)
    cycle_index = draw_cycle_index(jax.random.fold_in(arg_keys[7], 71), 0)
    order_values = draw_order_values(jax.random.fold_in(arg_keys[7], 71), 0)
    block_lengths = uneven(arg_keys[4], N_RADIAL, DEG, BLOCK_CAP, 2).astype(jnp.int32)
    legendre = gaussian(arg_keys[5], (ORDERS, DEG, CYCLES), (CYCLES * NPHI) ** -0.5, 0.0078125, ((0, 8),))
    bessel = bell_draw_with(arg_keys[6], (SHELLS, DEG, NMODES), SHELLS ** -0.5, 2.0, ((0, 32), (2, 8)), (0, 1, 32, 2.75))
    return dict(density=density, footprint=footprint, cycle_index=cycle_index, order_values=order_values, block_lengths=block_lengths, legendre=legendre, bessel=bessel)


def phase_table(nphi, order_values):
    pixel = lax.iota(jnp.int32, nphi)
    turns = (pixel[:, None] * 2 * order_values[None, :]) % (2 * nphi)
    angle = turns.astype(jnp.float32) * (math.pi / nphi)
    return jnp.concatenate([jnp.cos(angle), -jnp.sin(angle)], axis=1)


def latitude_twist(cycle_index, order_values, nphi):
    parity = (cycle_index - NSIDE + 1) % 2
    turns = (order_values[None, :] * (2 - parity)[:, None]) % (2 * nphi)
    angle = turns.astype(jnp.float32) * (math.pi / nphi)
    return jnp.cos(angle), jnp.sin(angle)


def reference(density, footprint, cycle_index, order_values, block_lengths, legendre, bessel):
    pixels = (density * footprint.astype(jnp.float32)).reshape(SHELLS * CYCLES, NPHI)
    spectra = jnp.dot(pixels, phase_table(NPHI, order_values), precision=lax.Precision.HIGHEST)
    spectra = spectra.reshape(SHELLS, CYCLES, 2, ORDERS)
    cos_t, sin_t = latitude_twist(cycle_index, order_values, NPHI)
    real0 = spectra[:, :, 0, :]
    imag0 = spectra[:, :, 1, :]
    real = real0 * cos_t + imag0 * sin_t
    imag = imag0 * cos_t - real0 * sin_t
    four = jnp.stack([real, imag], axis=2).astype(jnp.bfloat16)
    harmonic = jnp.einsum("mlr,srcm->smcl", legendre.astype(jnp.float32), four.astype(jnp.float32))
    degree = lax.iota(jnp.int32, DEG)
    keep = (degree[None, :] >= order_values[:, None]).astype(jnp.float32)
    harmonic = (harmonic * keep[None, :, None, :]).astype(jnp.bfloat16)
    starts = (jnp.cumsum(block_lengths) - block_lengths).astype(jnp.int32)
    offset = lax.iota(jnp.int32, BLOCK_CAP)
    rows = jnp.minimum(starts[:, None] + offset[None, :], DEG - 1).astype(jnp.int32)
    valid = (offset[None, :] < block_lengths[:, None]).astype(jnp.float32)

    def one_block(pair):
        block_rows, block_keep = pair
        radial_rows = jnp.take(bessel, block_rows, axis=1).astype(jnp.float32)
        coeffs = jnp.take(harmonic, block_rows, axis=3).astype(jnp.float32) * block_keep
        result = jnp.einsum("skn,smck->kncm", radial_rows, coeffs)
        return result.reshape(BLOCK_CAP, NMODES, 2 * ORDERS).astype(jnp.bfloat16)

    blocks = lax.map(one_block, (rows, valid))
    return blocks.reshape(SLOTS, NMODES, 2 * ORDERS)
```

```python
import math

import jax
import jax.numpy as jnp
from jax import lax
from jax.experimental import pallas as pl
from jax.experimental.pallas import tpu as pltpu
from jax.sharding import PartitionSpec as P

NSIDE = 1024
F32 = jnp.float32
BF16 = jnp.bfloat16
VMEM_LIMIT = 40 * 1024 * 1024

SMEM_SPEC = pl.BlockSpec(memory_space=pltpu.SMEM)
VMEM_SPEC = pl.BlockSpec(memory_space=pltpu.VMEM)
ANY_SPEC = pl.BlockSpec(memory_space=pl.ANY)


def params():
    return pltpu.CompilerParams(vmem_limit_bytes=VMEM_LIMIT)


def cos_sin(turns):
    quarter = (turns + 1024) >> 11
    x = (turns - (quarter << 11)).astype(F32) * (math.pi / 4096)
    z = x * x
    s = x + x * z * (-1.6666654611e-1 + z * (8.3321608736e-3 + z * -1.9515295891e-4))
    c = 1.0 - 0.5 * z + z * z * (4.166664568298827e-2 + z * (-1.388731625493765e-3 + z * 2.443315711809948e-5))
    odd = (quarter & 1) == 1
    even_sign = jnp.where((quarter & 2) == 2, -1.0, 1.0)
    cos = jnp.where(odd, -s, c) * even_sign
    sin = jnp.where(odd, c, s) * even_sign
    return cos, sin


def dft_kernel(where_ref, cycle_ref, order_ref, density_ref, footprint_ref, out_ref):
    rows, nphi = density_ref.shape
    order = order_ref[...]
    lane = lax.broadcasted_iota(jnp.int32, (1, 128), 1)
    part = (lane >> 3) & 1
    sixty_four = lax.broadcasted_iota(jnp.int32, (64, 128), 0)
    pa, qa = cos_sin((sixty_four * 128 * order + 2048 * part) & 8191)
    qa = -qa
    cb, sb = cos_sin((sixty_four * 2 * order) & 8191)
    total = jnp.zeros((2 * rows, 256), F32)
    for chunk in range(nphi // 256):
        tables = []
        for a in range(4 * chunk, 4 * chunk + 4):
            tables.append(pa[a : a + 1] * cb + qa[a : a + 1] * sb)
        table = jnp.concatenate(tables, axis=0)
        high = table.astype(BF16)
        low = (table - high.astype(F32)).astype(BF16)
        cut = slice(256 * chunk, 256 * chunk + 256)
        pixels = density_ref[:, cut] * footprint_ref[:, cut].astype(F32)
        p_high = pixels.astype(BF16)
        p_low = (pixels - p_high.astype(F32)).astype(BF16)
        total = total + jnp.dot(
            jnp.concatenate([p_high, p_low], axis=0),
            jnp.concatenate([high, low], axis=1),
            preferred_element_type=F32,
        )
    x = total[:rows, :128] + (total[:rows, 128:] + total[rows:, :128])
    row = lax.broadcasted_iota(jnp.int32, (rows, 128), 0)
    cycle = jnp.zeros((rows, 128), jnp.int32)
    for r in range(rows):
        cycle = jnp.where(row == r, cycle_ref[r], cycle)
    parity = (cycle - (NSIDE - 1)) & 1
    cos_t, sin_t = cos_sin((order * (2 - parity)) & 8191)
    other = jnp.where(part == 0, pltpu.roll(x, 120, 1), -pltpu.roll(x, 8, 1))
    four = (x * cos_t + other * sin_t).astype(BF16)
    lanes = lax.broadcasted_iota(jnp.int32, (rows, 128), 1)
    place = (lanes == row + rows * where_ref[1]).astype(BF16)
    out_ref[...] = lax.dot_general(four, place, (((0,), (0,)), ((), ())), preferred_element_type=F32).astype(BF16)


def send_kernel(lengths_ref, bessel_ref, out_ref, wide_ref):
    deg, modes = bessel_ref.shape
    blocks = out_ref.shape[0]
    wide_ref[pl.ds(0, deg), pl.ds(0, modes)] = bessel_ref[...].astype(F32)
    wide_ref[pl.ds(deg, 128), :] = jnp.zeros((128, 128), F32)

    def step(k, start):
        low = wide_ref[pl.ds(start, 64), :]
        high = wide_ref[pl.ds(start + 64, 64), :]
        lane = lax.broadcasted_iota(jnp.int32, (64, 128), 1)
        out_ref[k] = jnp.where(lane < 64, low, pltpu.roll(high, 64, 1)).astype(BF16)
        return start + lengths_ref[k]

    lax.fori_loop(0, blocks, step, jnp.int32(0))


def block_start(lengths_ref, block):
    return lax.fori_loop(0, block, lambda k, total: total + lengths_ref[k], jnp.int32(0))


def rows_kernel(where_ref, lengths_ref, legendre_ref, out_ref, window_ref, wide_ref, sem):
    deg = legendre_ref.shape[1]
    window = window_ref.shape[1]
    start = block_start(lengths_ref, where_ref[0])
    base = jnp.minimum((start // 16) * 16, deg - window)
    base = pl.multiple_of(base, 16)
    copy = pltpu.make_async_copy(legendre_ref.at[:, pl.ds(base, window), :], window_ref, sem)
    copy.start()
    copy.wait()
    shift = start - base
    wide_ref[pl.ds(window, 128), :] = jnp.zeros((128, 128), F32)
    for q in range(out_ref.shape[0]):
        wide_ref[pl.ds(0, window), :] = window_ref[q].astype(F32)
        out_ref[q] = wide_ref[pl.ds(shift, 128), :].astype(BF16)


def harmonic_kernel(where_ref, lengths_ref, order_ref, four_ref, rows_ref, out_ref, four32_ref, out32_ref):
    four32_ref[...] = four_ref[...].astype(F32)
    start = block_start(lengths_ref, where_ref[0])
    lane = lax.broadcasted_iota(jnp.int32, (32, 128), 1)
    degree = start + lax.broadcasted_iota(jnp.int32, (32, 128), 0) + 32 * (lane >> 5)
    group = lane >> 5
    for q in range(8):
        order = order_ref[8 * where_ref[1] + q]
        for c in range(2):
            one = four32_ref[pl.ds(c * 8 + q, 32, stride=16), :]
            four = jnp.concatenate([one] * 4, axis=0).astype(BF16)
            full = lax.dot_general(rows_ref[q], four, (((1,), (1,)), ((), ())), preferred_element_type=F32)
            packed = full[96:128]
            for j in range(3):
                packed = jnp.where(group == j, full[32 * j : 32 * j + 32], packed)
            packed = jnp.where(degree >= order, packed, 0.0)
            out32_ref[pl.ds(c * 8 + q, 32, stride=16), :] = packed
    out_ref[...] = out32_ref[...].astype(BF16)


def radial_kernel(where_ref, lengths_ref, recv_ref, out_ref, wide_ref):
    length = lengths_ref[where_ref[0]]
    wide_ref[...] = recv_ref[...].astype(F32)
    half = lax.broadcasted_iota(jnp.int32, (32, 128), 1) >> 6
    zero = jnp.zeros((32, 128), F32)

    def step(g, carry):
        turned = []
        for odd in range(2):
            x = wide_ref[pl.ds(g + 32 * odd, 32, stride=64), :]
            p = 64 * half + 32 * odd + g
            x = jnp.where(p < length, x, 0.0)
            low = jnp.where(half == 0, x, 0.0)
            high = jnp.where(half == 1, x, 0.0)
            pieces = [zero, low, zero, high] if odd else [low, zero, high, zero]
            turned.append(jnp.transpose(jnp.concatenate(pieces, axis=0)))
        even, other = turned
        out_ref[g] = jnp.concatenate([even[:64], other[:64], even[64:], other[64:]], axis=0).astype(BF16)
        return carry

    lax.fori_loop(0, 32, step, 0)


def final_kernel(radial_ref, harmonic_ref, out_ref):
    for g in range(radial_ref.shape[0]):
        h = harmonic_ref[:, g].astype(F32)
        right = jnp.concatenate([h[:, :8].reshape(64, 128), h[:, 8:].reshape(64, 128)], axis=0).astype(BF16)
        result = lax.dot_general(radial_ref[g], right, (((1,), (1,)), ((), ())), preferred_element_type=F32)
        out_ref[:, g] = result.reshape(4, 64, 128).astype(BF16)


def on_device(density, footprint, cycle_index, order_values, block_lengths, legendre, bessel):
    shape = jax.ShapeDtypeStruct
    rows, nphi = density.shape[1:]
    deg, modes = bessel.shape[1:]
    where = jnp.stack([lax.axis_index("radial"), lax.axis_index("shell")]).astype(jnp.int32)
    order_lanes = jnp.broadcast_to(order_values.reshape(8, 1, 8), (8, 2, 8)).reshape(1, 128)

    four = pl.pallas_call(
        dft_kernel,
        out_shape=shape((128, 128), BF16),
        in_specs=[SMEM_SPEC, SMEM_SPEC, VMEM_SPEC, VMEM_SPEC, VMEM_SPEC],
        out_specs=VMEM_SPEC,
        compiler_params=params(),
        name="dft",
    )(where, cycle_index, order_lanes, density.reshape(rows, nphi), footprint.reshape(rows, nphi))

    send = pl.pallas_call(
        send_kernel,
        out_shape=shape((32, 64, 128), BF16),
        in_specs=[SMEM_SPEC, VMEM_SPEC],
        out_specs=VMEM_SPEC,
        scratch_shapes=[pltpu.VMEM((deg + 128, 128), F32)],
        compiler_params=params(),
        name="bessel_send",
    )(block_lengths, bessel.reshape(deg, modes))
    recv = lax.all_to_all(send, "radial", split_axis=0, concat_axis=0, tiled=True)

    leg_rows = pl.pallas_call(
        rows_kernel,
        out_shape=shape((8, 128, 128), BF16),
        in_specs=[SMEM_SPEC, SMEM_SPEC, ANY_SPEC],
        out_specs=VMEM_SPEC,
        scratch_shapes=[pltpu.VMEM((8, 144, 128), BF16), pltpu.VMEM((144 + 128, 128), F32), pltpu.SemaphoreType.DMA],
        compiler_params=params(),
        name="legendre_rows",
    )(where, block_lengths, legendre)

    by_order = lax.all_to_all(four.reshape(8, 16, 128), "shell", split_axis=0, concat_axis=0, tiled=True)
    mine = jnp.sum(by_order, axis=0, dtype=F32).astype(BF16)
    every_shell = lax.all_to_all(jnp.broadcast_to(mine[None], (32, 16, 128)), "radial", split_axis=0, concat_axis=0, tiled=True)

    harmonic = pl.pallas_call(
        harmonic_kernel,
        out_shape=shape((512, 128), BF16),
        in_specs=[SMEM_SPEC, SMEM_SPEC, SMEM_SPEC, VMEM_SPEC, VMEM_SPEC],
        out_specs=VMEM_SPEC,
        scratch_shapes=[pltpu.VMEM((512, 128), F32), pltpu.VMEM((512, 128), F32)],
        compiler_params=params(),
        name="harmonic",
    )(where, block_lengths, order_values, every_shell.reshape(512, 128), leg_rows)
    every_order = lax.all_to_all(jnp.broadcast_to(harmonic[None], (8, 512, 128)), "shell", split_axis=0, concat_axis=0, tiled=True)

    radial = pl.pallas_call(
        radial_kernel,
        out_shape=shape((32, 256, 128), BF16),
        in_specs=[SMEM_SPEC, SMEM_SPEC, VMEM_SPEC],
        out_specs=VMEM_SPEC,
        scratch_shapes=[pltpu.VMEM((2048, 128), F32)],
        compiler_params=params(),
        name="radial_rows",
    )(where, block_lengths, recv.reshape(2048, 128))

    step = 4
    out = pl.pallas_call(
        final_kernel,
        out_shape=shape((4, 32, 64, 128), BF16),
        grid=(32 // step,),
        in_specs=[
            pl.BlockSpec((step, 256, 128), lambda g: (g, 0, 0)),
            pl.BlockSpec((8, step, 16, 128), lambda g: (0, g, 0, 0)),
        ],
        out_specs=pl.BlockSpec((4, step, 64, 128), lambda g: (0, g, 0, 0)),
        compiler_params=params(),
        name="combine",
    )(radial, every_order.reshape(8, 32, 16, 128))
    return out.reshape(128, modes, 128)


def solution(mesh):
    return jax.shard_map(
        on_device,
        mesh=mesh,
        in_specs=(
            P("radial", "shell", None),
            P("radial", "shell", None),
            P("shell"),
            P(),
            P(),
            P("shell", None, None),
            P("radial", None, "shell"),
        ),
        out_specs=P("radial", "shell", None),
        check_vma=False,
    )
```

```python
import math

import jax
import jax.numpy as jnp
from jax import lax
from jax.experimental import pallas as pl
from jax.experimental.pallas import tpu as pltpu
from jax.sharding import PartitionSpec as P

NSIDE = 1024
F32 = jnp.float32
BF16 = jnp.bfloat16
VMEM_LIMIT = 24 * 1024 * 1024

SMEM_SPEC = pl.BlockSpec(memory_space=pltpu.SMEM)
VMEM_SPEC = pl.BlockSpec(memory_space=pltpu.VMEM)
ANY_SPEC = pl.BlockSpec(memory_space=pl.ANY)
HBM_SPEC = pl.BlockSpec(memory_space=pltpu.HBM)


def params():
    return pltpu.CompilerParams(vmem_limit_bytes=VMEM_LIMIT)


def cost(microseconds, transferred):
    return pl.CostEstimate(flops=microseconds * 500_000_000, bytes_accessed=transferred, transcendentals=0)


def cos_sin(turns):
    quarter = (turns + 1024) >> 11
    x = (turns - (quarter << 11)).astype(F32) * (math.pi / 4096)
    z = x * x
    s = x + x * z * (-1.6666654611e-1 + z * (8.3321608736e-3 + z * -1.9515295891e-4))
    c = 1.0 - 0.5 * z + z * z * (4.166664568298827e-2 + z * (-1.388731625493765e-3 + z * 2.443315711809948e-5))
    odd = (quarter & 1) == 1
    even_sign = jnp.where((quarter & 2) == 2, -1.0, 1.0)
    cos = jnp.where(odd, -s, c) * even_sign
    sin = jnp.where(odd, c, s) * even_sign
    return cos, sin


def dft_kernel(cycle_hbm, order_hbm, density_hbm, footprint_hbm, out_ref, cycle_ref, order_ref, density_ref, footprint_ref, sems):
    _, rows, nphi = density_ref.shape
    copies = [
        pltpu.make_async_copy(order_hbm, order_ref, sems.at[0]),
        pltpu.make_async_copy(cycle_hbm, cycle_ref, sems.at[1]),
        pltpu.make_async_copy(density_hbm, density_ref, sems.at[2]),
        pltpu.make_async_copy(footprint_hbm, footprint_ref, sems.at[3]),
    ]
    for copy in copies:
        copy.start()
    copies[0].wait()
    lane = lax.broadcasted_iota(jnp.int32, (1, 128), 1)
    part = (lane >> 3) & 1
    slot = ((lane >> 4) << 3) + (lane & 7)
    order = jnp.zeros((1, 128), jnp.int32)
    for q in range(64):
        order = jnp.where(slot == q, order_ref[q], order)
    sixty_four = lax.broadcasted_iota(jnp.int32, (64, 128), 0)
    pa, qa = cos_sin((sixty_four * 128 * order + 2048 * part) & 8191)
    qa = -qa
    cb, sb = cos_sin((sixty_four * 2 * order) & 8191)
    for copy in copies[1:]:
        copy.wait()
    total = jnp.zeros((2 * rows, 256), F32)
    for chunk in range(nphi // 256):
        tables = []
        for a in range(4 * chunk, 4 * chunk + 4):
            tables.append(pa[a : a + 1] * cb + qa[a : a + 1] * sb)
        table = jnp.concatenate(tables, axis=0)
        high = table.astype(BF16)
        low = (table - high.astype(F32)).astype(BF16)
        cut = slice(256 * chunk, 256 * chunk + 256)
        pixels = density_ref[0, :, cut] * footprint_ref[0, :, cut].astype(F32)
        p_high = pixels.astype(BF16)
        p_low = (pixels - p_high.astype(F32)).astype(BF16)
        total = total + jnp.dot(
            jnp.concatenate([p_high, p_low], axis=0),
            jnp.concatenate([high, low], axis=1),
            preferred_element_type=F32,
        )
    x = total[:rows, :128] + (total[:rows, 128:] + total[rows:, :128])
    row = lax.broadcasted_iota(jnp.int32, (rows, 128), 0)
    cycle = jnp.zeros((rows, 128), jnp.int32)
    for r in range(rows):
        cycle = jnp.where(row == r, cycle_ref[r], cycle)
    parity = (cycle - (NSIDE - 1)) & 1
    cos_t, sin_t = cos_sin((order * (2 - parity)) & 8191)
    other = jnp.where(part == 0, pltpu.roll(x, 120, 1), -pltpu.roll(x, 8, 1))
    four = (x * cos_t + other * sin_t).astype(BF16)
    lanes = lax.broadcasted_iota(jnp.int32, (rows, 128), 1)
    place = (lanes == row + rows * lax.axis_index("shell")).astype(BF16)
    out_ref[...] = lax.dot_general(four, place, (((0,), (0,)), ((), ())), preferred_element_type=F32).astype(BF16)


def send_kernel(lengths_ref, bessel_ref, out_ref, wide_ref):
    modes, deg = bessel_ref.shape
    blocks = out_ref.shape[0]
    wide_ref[:, pl.ds(0, deg)] = bessel_ref[...].astype(F32)
    wide_ref[:, pl.ds(deg, 256)] = jnp.zeros((modes, 256), F32)
    lane = lax.broadcasted_iota(jnp.int32, (modes, 128), 1)

    def step(k, start):
        base = pl.multiple_of((start >> 7) << 7, 128)
        shift = start - base
        back = (128 - shift) & 127
        low = pltpu.roll(wide_ref[:, pl.ds(base, 128)], back, 1)
        high = pltpu.roll(wide_ref[:, pl.ds(base + 128, 128)], back, 1)
        out_ref[k, 16:, :] = jnp.where(lane < 128 - shift, low, high).astype(BF16)
        return start + lengths_ref[k]

    lax.fori_loop(0, blocks, step, jnp.int32(0), unroll=4)


def fill_kernel(parts_ref, send_ref, out_ref, tile_ref, sem):
    total = parts_ref[0].astype(F32)
    for h in range(1, parts_ref.shape[0]):
        total = total + parts_ref[h].astype(F32)
    tile_ref[...] = jnp.broadcast_to(total.astype(BF16)[None], tile_ref.shape)
    copy = pltpu.make_async_copy(tile_ref, out_ref.at[:, pl.ds(0, 16), :], sem)
    copy.start()
    copy.wait()


def block_start(lengths_ref, block):
    return lax.fori_loop(0, block, lambda k, total: total + lengths_ref[k], jnp.int32(0))


def rows_kernel(lengths_ref, legendre_ref, out_ref, window_ref, wide_ref, sem):
    deg = legendre_ref.shape[1]
    window = window_ref.shape[1]
    start = block_start(lengths_ref, lax.axis_index("radial"))
    base = jnp.minimum((start >> 4) << 4, deg - window)
    base = pl.multiple_of(base, 16)
    copy = pltpu.make_async_copy(legendre_ref.at[:, pl.ds(base, window), :], window_ref, sem)
    copy.start()
    copy.wait()
    shift = start - base
    wide_ref[pl.ds(window, 128), :] = jnp.zeros((128, 128), F32)
    for q in range(out_ref.shape[0]):
        wide_ref[pl.ds(0, window), :] = window_ref[q].astype(F32)
        out_ref[q] = wide_ref[pl.ds(shift, 128), :].astype(BF16)


def harmonic_kernel(lengths_ref, order_ref, recv_ref, rows_ref, out_ref, four32_ref, out32_ref):
    four32_ref[...] = recv_ref[:, :16].astype(F32).reshape(512, 128)
    start = block_start(lengths_ref, lax.axis_index("radial"))
    lane = lax.broadcasted_iota(jnp.int32, (32, 128), 1)
    degree = start + lax.broadcasted_iota(jnp.int32, (32, 128), 0) + 32 * (lane >> 5)
    group = lane >> 5
    for q in range(8):
        order = order_ref[8 * lax.axis_index("shell") + q]
        for c in range(2):
            one = four32_ref[pl.ds(c * 8 + q, 32, stride=16), :]
            four = jnp.concatenate([one] * 4, axis=0).astype(BF16)
            full = lax.dot_general(rows_ref[q], four, (((1,), (1,)), ((), ())), preferred_element_type=F32)
            packed = full[96:128]
            for j in range(3):
                packed = jnp.where(group == j, full[32 * j : 32 * j + 32], packed)
            packed = jnp.where(degree >= order, packed, 0.0)
            out32_ref[pl.ds(c * 8 + q, 32, stride=16), :] = packed
    out_ref[...] = out32_ref[...].astype(BF16)


def radial_kernel(lengths_ref, recv_ref, out_ref, wide_ref, turned_ref):
    length = lengths_ref[lax.axis_index("radial")]
    modes = 64
    wide_ref[...] = recv_ref[:, 16:].astype(F32).reshape(32 * modes, 128)
    slot = lax.broadcasted_iota(jnp.int32, (128, 128), 1)
    group = lax.broadcasted_iota(jnp.int32, (128, 128), 0)
    keep = ((slot >> 5) == (group >> 5)) & (slot < length)

    def step(n, carry):
        x = wide_ref[pl.ds(n, 32, stride=modes), :]
        x = jnp.where(keep, jnp.concatenate([x] * 4, axis=0), 0.0)
        turned = jnp.transpose(x)
        for j in range(4):
            turned_ref[pl.ds(j * modes + n, 32, stride=4 * modes), :] = turned[32 * j : 32 * j + 32]
        return carry

    lax.fori_loop(0, modes, step, 0, unroll=2)
    for g in range(32):
        out_ref[g] = turned_ref[pl.ds(g * 256, 256), :].astype(BF16)


def final_kernel(radial_ref, *refs):
    pieces, out_ref, right_ref = refs[:8], refs[8], refs[9]
    mine = lax.axis_index("shell")
    steps = out_ref.shape[1]
    for i in range(steps):
        g = pl.program_id(0) * steps + i
        for d in range(8):
            h = mine ^ d
            piece = pieces[d][pl.ds(pl.multiple_of(g * 16, 16), 16), :].astype(F32)
            right_ref[i, 0, h] = piece[:8]
            right_ref[i, 1, h] = piece[8:]
        right = right_ref[i].reshape(128, 128).astype(BF16)
        result = lax.dot_general(radial_ref[g], right, (((1,), (1,)), ((), ())), preferred_element_type=F32)
        out_ref[:, i] = result.reshape(4, 64, 128).astype(BF16)


def on_device(density, footprint, cycle_index, order_values, block_lengths, legendre, bessel):
    shape = jax.ShapeDtypeStruct
    rows, nphi = density.shape[1:]
    deg, modes = bessel.shape[1:]
    dma = pltpu.SemaphoreType.DMA

    four = pl.pallas_call(
        dft_kernel,
        out_shape=shape((128, 128), BF16),
        in_specs=[HBM_SPEC] * 4,
        out_specs=VMEM_SPEC,
        scratch_shapes=[
            pltpu.SMEM((rows,), jnp.int32),
            pltpu.SMEM((64,), jnp.int32),
            pltpu.VMEM((1, rows, nphi), F32),
            pltpu.VMEM((1, rows, nphi), jnp.int32),
            dma((4,)),
        ],
        compiler_params=params(),
        cost_estimate=cost(2, 1 << 19),
        name="dft",
    )(cycle_index, order_values, density, footprint)
    by_order = lax.all_to_all(four.reshape(8, 16, 128), "shell", split_axis=0, concat_axis=0, tiled=True)

    send = pl.pallas_call(
        send_kernel,
        out_shape=shape((32, 16 + modes, 128), BF16),
        in_specs=[SMEM_SPEC, VMEM_SPEC],
        out_specs=VMEM_SPEC,
        scratch_shapes=[pltpu.VMEM((modes, deg + 256), F32)],
        compiler_params=params(),
        cost_estimate=cost(2, 1 << 20),
        name="bessel_send",
    )(block_lengths, jnp.swapaxes(bessel, 1, 2).reshape(modes, deg))
    send = pl.pallas_call(
        fill_kernel,
        out_shape=shape(send.shape, BF16),
        in_specs=[VMEM_SPEC, ANY_SPEC],
        out_specs=ANY_SPEC,
        scratch_shapes=[pltpu.VMEM((32, 16, 128), BF16), dma],
        input_output_aliases={1: 0},
        compiler_params=params(),
        cost_estimate=cost(1, 1 << 17),
        name="fill",
    )(by_order, send)
    recv = lax.all_to_all(send, "radial", split_axis=0, concat_axis=0, tiled=True)

    leg_rows = pl.pallas_call(
        rows_kernel,
        out_shape=shape((8, 128, 128), BF16),
        in_specs=[SMEM_SPEC, HBM_SPEC],
        out_specs=VMEM_SPEC,
        scratch_shapes=[pltpu.VMEM((8, 144, 128), BF16), pltpu.VMEM((144 + 128, 128), F32), dma],
        compiler_params=params(),
        cost_estimate=cost(1, 1 << 19),
        name="legendre_rows",
    )(block_lengths, legendre)

    harmonic = pl.pallas_call(
        harmonic_kernel,
        out_shape=shape((512, 128), BF16),
        in_specs=[SMEM_SPEC, SMEM_SPEC, VMEM_SPEC, VMEM_SPEC],
        out_specs=VMEM_SPEC,
        scratch_shapes=[pltpu.VMEM((512, 128), F32), pltpu.VMEM((512, 128), F32)],
        compiler_params=params(),
        cost_estimate=cost(1, 1 << 19),
        name="harmonic",
    )(block_lengths, order_values, recv, leg_rows)

    def swap(x, d):
        return lax.ppermute(x, "shell", [(i, i ^ d) for i in range(8)])

    pieces = {0: harmonic}
    for d in (2, 6, 4):
        pieces[d] = swap(harmonic, d)
    for d in (0, 2, 6, 4):
        pieces[d + 1] = swap(pieces[d], 1)

    radial = pl.pallas_call(
        radial_kernel,
        out_shape=shape((32, 4 * modes, 128), BF16),
        in_specs=[SMEM_SPEC, VMEM_SPEC],
        out_specs=VMEM_SPEC,
        scratch_shapes=[pltpu.VMEM((32 * modes, 128), F32), pltpu.VMEM((128 * modes, 128), F32)],
        compiler_params=params(),
        cost_estimate=cost(5, 1 << 21),
        name="radial_rows",
    )(block_lengths, recv)

    step = 4
    out = pl.pallas_call(
        final_kernel,
        out_shape=shape((4, 32, modes, 128), BF16),
        grid=(32 // step,),
        in_specs=[VMEM_SPEC] * 9,
        out_specs=pl.BlockSpec((4, step, modes, 128), lambda g: (0, g, 0, 0)),
        scratch_shapes=[pltpu.VMEM((step, 2, 8, 8, 128), F32)],
        compiler_params=params(),
        cost_estimate=cost(4, 1 << 22),
        name="combine",
    )(radial, *[pieces[d] for d in range(8)])
    return out.reshape(128, modes, 128)


def solution(mesh):
    return jax.shard_map(
        on_device,
        mesh=mesh,
        in_specs=(
            P("radial", "shell", None),
            P("radial", "shell", None),
            P("shell"),
            P(),
            P(),
            P("shell", None, None),
            P("radial", None, "shell"),
        ),
        out_specs=P("radial", "shell", None),
        check_vma=False,
    )
```

```python
import math

import jax
import jax.numpy as jnp
from jax import lax
from jax.experimental import pallas as pl
from jax.experimental.pallas import tpu as pltpu
from jax.sharding import PartitionSpec as P

NSIDE = 1024
F32 = jnp.float32
BF16 = jnp.bfloat16
VMEM_LIMIT = 16 * 1024 * 1024
VMEM_WHOLE = 64 * 1024 * 1024
CHUNKS = 4

SMEM_SPEC = pl.BlockSpec(memory_space=pltpu.SMEM)
VMEM_SPEC = pl.BlockSpec(memory_space=pltpu.VMEM)
ANY_SPEC = pl.BlockSpec(memory_space=pl.ANY)
HBM_SPEC = pl.BlockSpec(memory_space=pltpu.HBM)


def params(limit=VMEM_LIMIT):
    return pltpu.CompilerParams(vmem_limit_bytes=limit)


def cost(microseconds, transferred):
    return pl.CostEstimate(flops=microseconds * 500_000_000, bytes_accessed=transferred, transcendentals=0)


def cos_sin(turns):
    quarter = (turns + 1024) >> 11
    x = (turns - (quarter << 11)).astype(F32) * (math.pi / 4096)
    z = x * x
    s = x + x * z * (-1.6666654611e-1 + z * (8.3321608736e-3 + z * -1.9515295891e-4))
    c = 1.0 - 0.5 * z + z * z * (4.166664568298827e-2 + z * (-1.388731625493765e-3 + z * 2.443315711809948e-5))
    odd = (quarter & 1) == 1
    even_sign = jnp.where((quarter & 2) == 2, -1.0, 1.0)
    cos = jnp.where(odd, -s, c) * even_sign
    sin = jnp.where(odd, c, s) * even_sign
    return cos, sin


def dft_kernel(cycle_hbm, order_hbm, density_hbm, footprint_hbm, out_ref, cycle_ref, order_ref, density_ref, footprint_ref, sems):
    _, rows, nphi = density_ref.shape
    copies = [
        pltpu.make_async_copy(order_hbm, order_ref, sems.at[0]),
        pltpu.make_async_copy(cycle_hbm, cycle_ref, sems.at[1]),
        pltpu.make_async_copy(density_hbm, density_ref, sems.at[2]),
        pltpu.make_async_copy(footprint_hbm, footprint_ref, sems.at[3]),
    ]
    for copy in copies:
        copy.start()
    copies[0].wait()
    lane = lax.broadcasted_iota(jnp.int32, (1, 128), 1)
    part = (lane >> 3) & 1
    slot = ((lane >> 4) << 3) + (lane & 7)
    order = jnp.zeros((1, 128), jnp.int32)
    for q in range(64):
        order = jnp.where(slot == q, order_ref[q], order)
    sixty_four = lax.broadcasted_iota(jnp.int32, (64, 128), 0)
    pa, qa = cos_sin((sixty_four * 128 * order + 2048 * part) & 8191)
    qa = -qa
    cb, sb = cos_sin((sixty_four * 2 * order) & 8191)
    for copy in copies[1:]:
        copy.wait()
    total = jnp.zeros((2 * rows, 256), F32)
    for chunk in range(nphi // 256):
        tables = []
        for a in range(4 * chunk, 4 * chunk + 4):
            tables.append(pa[a : a + 1] * cb + qa[a : a + 1] * sb)
        table = jnp.concatenate(tables, axis=0)
        high = table.astype(BF16)
        low = (table - high.astype(F32)).astype(BF16)
        cut = slice(256 * chunk, 256 * chunk + 256)
        pixels = density_ref[0, :, cut] * footprint_ref[0, :, cut].astype(F32)
        p_high = pixels.astype(BF16)
        p_low = (pixels - p_high.astype(F32)).astype(BF16)
        total = total + jnp.dot(
            jnp.concatenate([p_high, p_low], axis=0),
            jnp.concatenate([high, low], axis=1),
            preferred_element_type=F32,
        )
    x = total[:rows, :128] + (total[:rows, 128:] + total[rows:, :128])
    row = lax.broadcasted_iota(jnp.int32, (rows, 128), 0)
    cycle = jnp.zeros((rows, 128), jnp.int32)
    for r in range(rows):
        cycle = jnp.where(row == r, cycle_ref[r], cycle)
    parity = (cycle - (NSIDE - 1)) & 1
    cos_t, sin_t = cos_sin((order * (2 - parity)) & 8191)
    other = jnp.where(part == 0, pltpu.roll(x, 120, 1), -pltpu.roll(x, 8, 1))
    four = (x * cos_t + other * sin_t).astype(BF16)
    lanes = lax.broadcasted_iota(jnp.int32, (rows, 128), 1)
    place = (lanes == row + rows * lax.axis_index("shell")).astype(BF16)
    out_ref[...] = lax.dot_general(four, place, (((0,), (0,)), ((), ())), preferred_element_type=F32).astype(BF16)


def send_kernel(lengths_ref, bessel_ref, out_ref, wide_ref):
    modes, deg = bessel_ref.shape
    blocks = out_ref.shape[0]
    wide_ref[:, pl.ds(0, deg)] = bessel_ref[...].astype(F32)
    wide_ref[:, pl.ds(deg, 256)] = jnp.zeros((modes, 256), F32)
    lane = lax.broadcasted_iota(jnp.int32, (modes, 128), 1)
    tile = lax.broadcasted_iota(jnp.int32, (16, 128), 1) >> 5

    def step(k, start):
        base = pl.multiple_of((start >> 7) << 7, 128)
        shift = start - base
        back = (128 - shift) & 127
        low = pltpu.roll(wide_ref[:, pl.ds(base, 128)], back, 1)
        high = pltpu.roll(wide_ref[:, pl.ds(base + 128, 128)], back, 1)
        block = jnp.where(lane < 128 - shift, low, high)
        for j in range(4):
            row = block[16 * j : 16 * j + 16]
            for m in range(4):
                if m != j:
                    row = jnp.where(tile == m, pltpu.roll(block[16 * m : 16 * m + 16], (32 * (m - j)) % 128, 1), row)
            out_ref[k, 16 + 16 * j : 32 + 16 * j, :] = row.astype(BF16)
        return start + lengths_ref[k]

    lax.fori_loop(0, blocks, step, jnp.int32(0), unroll=4)


def fill_kernel(parts_ref, send_ref, out_ref, tile_ref, sem):
    total = parts_ref[0].astype(F32)
    for h in range(1, parts_ref.shape[0]):
        total = total + parts_ref[h].astype(F32)
    tile_ref[...] = jnp.broadcast_to(total.astype(BF16)[None], tile_ref.shape)
    copy = pltpu.make_async_copy(tile_ref, out_ref.at[:, pl.ds(0, 16), :], sem)
    copy.start()
    copy.wait()


def block_start(lengths_ref, block):
    return lax.fori_loop(0, block, lambda k, total: total + lengths_ref[k], jnp.int32(0))


def rows_kernel(lengths_ref, legendre_ref, out_ref, window_ref, wide_ref, sem):
    deg = legendre_ref.shape[1]
    window = window_ref.shape[1]
    start = block_start(lengths_ref, lax.axis_index("radial"))
    base = jnp.minimum((start >> 4) << 4, deg - window)
    base = pl.multiple_of(base, 16)
    copy = pltpu.make_async_copy(legendre_ref.at[:, pl.ds(base, window), :], window_ref, sem)
    copy.start()
    copy.wait()
    shift = start - base
    wide_ref[pl.ds(window, 128), :] = jnp.zeros((128, 128), F32)
    for q in range(out_ref.shape[0]):
        wide_ref[pl.ds(0, window), :] = window_ref[q].astype(F32)
        out_ref[q] = wide_ref[pl.ds(shift, 128), :].astype(BF16)


def harmonic_kernel(lengths_ref, order_ref, recv_ref, rows_ref, out_ref, four32_ref, out32_ref):
    four32_ref[...] = recv_ref[:, :16].astype(F32).reshape(512, 128)
    start = block_start(lengths_ref, lax.axis_index("radial"))
    lane = lax.broadcasted_iota(jnp.int32, (32, 128), 1)
    degree = start + lax.broadcasted_iota(jnp.int32, (32, 128), 0) + 32 * (lane >> 5)
    group = lane >> 5
    for q in range(8):
        order = order_ref[8 * lax.axis_index("shell") + q]
        for c in range(2):
            one = four32_ref[pl.ds(c * 8 + q, 32, stride=16), :]
            four = jnp.concatenate([one] * 4, axis=0).astype(BF16)
            full = lax.dot_general(rows_ref[q], four, (((1,), (1,)), ((), ())), preferred_element_type=F32)
            packed = full[96:128]
            for j in range(3):
                packed = jnp.where(group == j, full[32 * j : 32 * j + 32], packed)
            packed = jnp.where(degree >= order, packed, 0.0)
            out32_ref[pl.ds(c * 8 + q, 32, stride=16), :] = packed
    out_ref[...] = out32_ref[...].astype(BF16)


def radial_kernel(lengths_ref, recv_ref, out_ref, wide_ref, turned_ref):
    length = lengths_ref[lax.axis_index("radial")]
    wide_ref[...] = recv_ref[:, 16:].astype(F32).reshape(wide_ref.shape)
    lane = lax.broadcasted_iota(jnp.int32, (128, 128), 1)
    row = lax.broadcasted_iota(jnp.int32, (128, 128), 0)
    keep = 32 * (row >> 5) + (lane & 31) < length

    def step(a, carry):
        x = jnp.concatenate([wide_ref[pl.ds(16 * j + a, 32, stride=64), :] for j in range(4)], axis=0)
        turned = jnp.transpose(jnp.where(keep, x, 0.0))
        for m in range(4):
            turned_ref[pl.ds(16 * m + a, 32, stride=64), :] = turned[32 * m : 32 * m + 32]
        return carry

    lax.fori_loop(0, 16, step, 0, unroll=4)
    out_ref[...] = turned_ref[...].astype(BF16).reshape(out_ref.shape)


def final_kernel(radial_ref, *refs):
    pieces, out_ref, right_ref, block_ref, sems = refs[:8], refs[8], refs[9], refs[10], refs[11]
    mine = lax.axis_index("shell")
    group = lax.broadcasted_iota(jnp.int32, (64, 128), 1) >> 5
    zero = jnp.zeros((64, 128), BF16)
    per = 32 // CHUNKS
    copies = []
    for g in range(32):
        for d in range(8):
            h = mine ^ d
            piece = pieces[d][g * 16 : g * 16 + 16, :].astype(F32)
            right_ref[g, 0, h] = piece[:8]
            right_ref[g, 1, h] = piece[8:]
        right = right_ref[g].reshape(128, 128).astype(BF16)
        left = jnp.concatenate([jnp.where(group == j, radial_ref[g], zero) for j in range(4)], axis=0)
        result = lax.dot_general(left, right, (((1,), (1,)), ((), ())), preferred_element_type=F32)
        block_ref[:, g] = result.reshape(4, 64, 128).astype(BF16)
        if g % per == per - 1:
            part = pl.ds(g + 1 - per, per)
            copy = pltpu.make_async_copy(block_ref.at[:, part], out_ref.at[:, part], sems.at[g // per])
            copy.start()
            copies.append(copy)
    for copy in copies:
        copy.wait()


def on_device(density, footprint, cycle_index, order_values, block_lengths, legendre, bessel):
    shape = jax.ShapeDtypeStruct
    rows, nphi = density.shape[1:]
    deg, modes = bessel.shape[1:]
    dma = pltpu.SemaphoreType.DMA

    four = pl.pallas_call(
        dft_kernel,
        out_shape=shape((128, 128), BF16),
        in_specs=[HBM_SPEC] * 4,
        out_specs=VMEM_SPEC,
        scratch_shapes=[
            pltpu.SMEM((rows,), jnp.int32),
            pltpu.SMEM((64,), jnp.int32),
            pltpu.VMEM((1, rows, nphi), F32),
            pltpu.VMEM((1, rows, nphi), jnp.int32),
            dma((4,)),
        ],
        compiler_params=params(VMEM_WHOLE),
        cost_estimate=cost(2, 1 << 19),
        name="dft",
    )(cycle_index, order_values, density, footprint)
    by_order = lax.all_to_all(four.reshape(8, 16, 128), "shell", split_axis=0, concat_axis=0, tiled=True)

    send = pl.pallas_call(
        send_kernel,
        out_shape=shape((32, 16 + modes, 128), BF16),
        in_specs=[SMEM_SPEC, VMEM_SPEC],
        out_specs=VMEM_SPEC,
        scratch_shapes=[pltpu.VMEM((modes, deg + 256), F32)],
        compiler_params=params(),
        cost_estimate=cost(2, 1 << 20),
        name="bessel_send",
    )(block_lengths, jnp.swapaxes(bessel, 1, 2).reshape(modes, deg))
    send = pl.pallas_call(
        fill_kernel,
        out_shape=shape(send.shape, BF16),
        in_specs=[VMEM_SPEC, ANY_SPEC],
        out_specs=ANY_SPEC,
        scratch_shapes=[pltpu.VMEM((32, 16, 128), BF16), dma],
        input_output_aliases={1: 0},
        compiler_params=params(),
        cost_estimate=cost(1, 1 << 17),
        name="fill",
    )(by_order, send)
    recv = lax.all_to_all(send, "radial", split_axis=0, concat_axis=0, tiled=True)

    leg_rows = pl.pallas_call(
        rows_kernel,
        out_shape=shape((8, 128, 128), BF16),
        in_specs=[SMEM_SPEC, HBM_SPEC],
        out_specs=VMEM_SPEC,
        scratch_shapes=[pltpu.VMEM((8, 144, 128), BF16), pltpu.VMEM((144 + 128, 128), F32), dma],
        compiler_params=params(),
        cost_estimate=cost(1, 1 << 19),
        name="legendre_rows",
    )(block_lengths, legendre)

    harmonic = pl.pallas_call(
        harmonic_kernel,
        out_shape=shape((512, 128), BF16),
        in_specs=[SMEM_SPEC, SMEM_SPEC, VMEM_SPEC, VMEM_SPEC],
        out_specs=VMEM_SPEC,
        scratch_shapes=[pltpu.VMEM((512, 128), F32), pltpu.VMEM((512, 128), F32)],
        compiler_params=params(),
        cost_estimate=cost(1, 1 << 19),
        name="harmonic",
    )(block_lengths, order_values, recv, leg_rows)

    def swap(x, d):
        return lax.ppermute(x, "shell", [(i, i ^ d) for i in range(8)])

    pieces = {0: harmonic}
    for d in (2, 6, 4):
        pieces[d] = swap(harmonic, d)
    for d in (0, 2, 6, 4):
        pieces[d + 1] = swap(pieces[d], 1)

    radial = pl.pallas_call(
        radial_kernel,
        out_shape=shape((32, modes, 128), BF16),
        in_specs=[SMEM_SPEC, VMEM_SPEC],
        out_specs=VMEM_SPEC,
        scratch_shapes=[pltpu.VMEM((32 * modes, 128), F32), pltpu.VMEM((32 * modes, 128), F32)],
        compiler_params=params(),
        cost_estimate=cost(3, 1 << 20),
        name="radial_rows",
    )(block_lengths, recv)

    out = pl.pallas_call(
        final_kernel,
        out_shape=shape((4, 32, modes, 128), BF16),
        in_specs=[VMEM_SPEC] * 9,
        out_specs=HBM_SPEC,
        scratch_shapes=[pltpu.VMEM((32, 2, 8, 8, 128), F32), pltpu.VMEM((4, 32, modes, 128), BF16), dma((CHUNKS,))],
        compiler_params=params(),
        cost_estimate=cost(2, 1 << 22),
        name="combine",
    )(radial, *[pieces[d] for d in range(8)])
    return out.reshape(128, modes, 128)


def solution(mesh):
    return jax.shard_map(
        on_device,
        mesh=mesh,
        in_specs=(
            P("radial", "shell", None),
            P("radial", "shell", None),
            P("shell"),
            P(),
            P(),
            P("shell", None, None),
            P("radial", None, "shell"),
        ),
        out_specs=P("radial", "shell", None),
        check_vma=False,
    )
```

```python
import math

import jax
import jax.numpy as jnp
from jax import lax
from jax.experimental import pallas as pl
from jax.experimental.pallas import tpu as pltpu
from jax.sharding import PartitionSpec as P

NSIDE = 1024
F32 = jnp.float32
BF16 = jnp.bfloat16
VMEM_LIMIT = 16 * 1024 * 1024
VMEM_WHOLE = 64 * 1024 * 1024

SMEM_SPEC = pl.BlockSpec(memory_space=pltpu.SMEM)
VMEM_SPEC = pl.BlockSpec(memory_space=pltpu.VMEM)
HBM_SPEC = pl.BlockSpec(memory_space=pltpu.HBM)


def params(limit=VMEM_LIMIT):
    return pltpu.CompilerParams(vmem_limit_bytes=limit)


def cost(microseconds, transferred):
    return pl.CostEstimate(flops=microseconds * 500_000_000, bytes_accessed=transferred, transcendentals=0)


def split_start(start):
    base = pl.multiple_of((start >> 7) << 7, 128)
    return base, start - base


def cos_sin(turns):
    quarter = (turns + 1024) >> 11
    x = (turns - (quarter << 11)).astype(F32) * (math.pi / 4096)
    z = x * x
    s = x + x * z * (-1.6666654611e-1 + z * (8.3321608736e-3 + z * -1.9515295891e-4))
    c = 1.0 - 0.5 * z + z * z * (4.166664568298827e-2 + z * (-1.388731625493765e-3 + z * 2.443315711809948e-5))
    odd = (quarter & 1) == 1
    even_sign = jnp.where((quarter & 2) == 2, -1.0, 1.0)
    cos = jnp.where(odd, -s, c) * even_sign
    sin = jnp.where(odd, c, s) * even_sign
    return cos, sin


def front_kernel(
    lengths_hbm, cycle_hbm, order_hbm, density_hbm, footprint_hbm, bessel_hbm, legendre_hbm, send_hbm, rows_hbm,
    lengths_ref, cycle_ref, order_ref, density_ref, footprint_ref, bessel_ref, low_ref, high_ref,
    block_ref, tile_ref, rows_ref, sems,
):
    _, rows, nphi = density_ref.shape
    modes, deg = bessel_ref.shape
    inputs = [
        (lengths_hbm, lengths_ref),
        (bessel_hbm, bessel_ref),
        (order_hbm, order_ref),
        (density_hbm, density_ref),
        (footprint_hbm, footprint_ref),
        (cycle_hbm, cycle_ref),
    ]
    copies = [pltpu.make_async_copy(source, target, sems.at[i]) for i, (source, target) in enumerate(inputs)]
    for copy in copies:
        copy.start()
    copies[0].wait()
    base, shift = split_start(block_start(lengths_ref))
    after = pl.multiple_of(jnp.minimum(base + 128, deg - 128), 128)
    windows = [
        pltpu.make_async_copy(legendre_hbm.at[:, pl.ds(base, 128), :], low_ref, sems.at[6]),
        pltpu.make_async_copy(legendre_hbm.at[:, pl.ds(after, 128), :], high_ref, sems.at[7]),
    ]
    for copy in windows:
        copy.start()
    copies[1].wait()
    lane = lax.broadcasted_iota(jnp.int32, (modes, 128), 1)
    tile = lax.broadcasted_iota(jnp.int32, (16, 128), 1) >> 5

    def step(k, start):
        base, shift = split_start(start)
        after = pl.multiple_of(jnp.minimum(base + 128, deg - 128), 128)
        block = jnp.where(lane >= shift, bessel_ref[:, pl.ds(base, 128)], bessel_ref[:, pl.ds(after, 128)])
        for j in range(4):
            row = block[16 * j : 16 * j + 16]
            for i in range(4):
                if i != j:
                    row = jnp.where(tile == i, pltpu.roll(block[16 * i : 16 * i + 16], (32 * (i - j)) % 128, 1), row)
            block_ref[k, 16 * j : 16 * j + 16, :] = row
        return start + lengths_ref[k]

    lax.fori_loop(0, block_ref.shape[0], step, jnp.int32(0), unroll=4)
    outputs = [pltpu.make_async_copy(block_ref, send_hbm.at[:, pl.ds(16, modes), :], sems.at[8])]
    outputs[0].start()

    for copy in windows:
        copy.wait()
    slot = lax.broadcasted_iota(jnp.int32, (128, 128), 0)
    for q in range(rows_ref.shape[0]):
        rows_ref[q] = jnp.where(slot >= shift, low_ref[q], high_ref[q])
    outputs.append(pltpu.make_async_copy(rows_ref, rows_hbm, sems.at[9]))
    outputs[1].start()

    for copy in copies[2:]:
        copy.wait()
    lane = lax.broadcasted_iota(jnp.int32, (1, 128), 1)
    part = (lane >> 5) & 1
    order_slot = 2 * (lane & 31) + (lane >> 6)
    order = jnp.zeros((1, 128), jnp.int32)
    for q in range(64):
        order = jnp.where(order_slot == q, order_ref[q], order)
    sixty_four = lax.broadcasted_iota(jnp.int32, (64, 128), 0)
    pa, qa = cos_sin((sixty_four * 128 * order + 2048 * part) & 8191)
    qa = -qa
    cb, sb = cos_sin((sixty_four * 2 * order) & 8191)
    total = jnp.zeros((2 * rows, 256), F32)
    for chunk in range(nphi // 256):
        tables = []
        for a in range(4 * chunk, 4 * chunk + 4):
            tables.append(pa[a : a + 1] * cb + qa[a : a + 1] * sb)
        table = jnp.concatenate(tables, axis=0)
        high = table.astype(BF16)
        low = (table - high.astype(F32)).astype(BF16)
        cut = slice(256 * chunk, 256 * chunk + 256)
        pixels = density_ref[0, :, cut] * footprint_ref[0, :, cut].astype(F32)
        p_high = pixels.astype(BF16)
        p_low = (pixels - p_high.astype(F32)).astype(BF16)
        total = total + jnp.dot(
            jnp.concatenate([p_high, p_low], axis=0),
            jnp.concatenate([high, low], axis=1),
            preferred_element_type=F32,
        )
    x = total[:rows, :128] + (total[:rows, 128:] + total[rows:, :128])
    row = lax.broadcasted_iota(jnp.int32, (rows, 128), 0)
    cycle = jnp.zeros((rows, 128), jnp.int32)
    for r in range(rows):
        cycle = jnp.where(row == r, cycle_ref[r], cycle)
    parity = (cycle - (NSIDE - 1)) & 1
    cos_t, sin_t = cos_sin((order * (2 - parity)) & 8191)
    other = jnp.where(part == 0, pltpu.roll(x, 96, 1), -pltpu.roll(x, 32, 1))
    four = (x * cos_t + other * sin_t).astype(BF16)
    tile_ref[...] = jnp.broadcast_to(four[None], tile_ref.shape)
    outputs.append(pltpu.make_async_copy(tile_ref, send_hbm.at[:, pl.ds(0, 16), :], sems.at[10]))
    outputs[2].start()
    for copy in outputs:
        copy.wait()


def turn_kernel(recv_ref, out_ref, wide_ref, turned_ref):
    wide_ref[...] = recv_ref[:, :16].astype(F32).reshape(512, 128)
    tile = lax.broadcasted_iota(jnp.int32, (32, 128), 1) >> 5
    for a in range(4):
        x = [wide_ref[pl.ds(4 * a + b, 32, stride=16), :] for b in range(4)]
        pieces = []
        for u in range(4):
            piece = x[u]
            for b in range(4):
                if b != u:
                    piece = jnp.where(tile == b, pltpu.roll(x[b], (32 * (b - u)) % 128, 1), piece)
            pieces.append(piece)
        turned = jnp.transpose(jnp.concatenate(pieces, axis=0))
        for b in range(4):
            turned_ref[pl.ds(4 * a + b, 32, stride=16), :] = turned[32 * b : 32 * b + 32]
    out_ref[...] = turned_ref[...].astype(BF16)


def block_start(lengths_ref):
    return lax.fori_loop(0, lax.axis_index("radial"), lambda k, total: total + lengths_ref[k], jnp.int32(0))


def radial_kernel(lengths_ref, recv_ref, out_ref, wide_ref, turned_ref):
    length = lengths_ref[lax.axis_index("radial")]
    start = block_start(lengths_ref)
    wide_ref[...] = recv_ref[:, 16:].astype(F32).reshape(wide_ref.shape)
    lane = lax.broadcasted_iota(jnp.int32, (128, 128), 1)
    row = lax.broadcasted_iota(jnp.int32, (128, 128), 0)
    slot = 32 * (row >> 5) + (lane & 31)
    keep = ((slot - start) & 127) < length

    def step(a, carry):
        x = jnp.concatenate([wide_ref[pl.ds(16 * j + a, 32, stride=64), :] for j in range(4)], axis=0)
        turned = jnp.transpose(jnp.where(keep, x, 0.0))
        for m in range(4):
            turned_ref[pl.ds(16 * m + a, 32, stride=64), :] = turned[32 * m : 32 * m + 32]
        return carry

    lax.fori_loop(0, 16, step, 0, unroll=4)
    out_ref[...] = turned_ref[...].astype(BF16).reshape(out_ref.shape)


def final_kernel(lengths_ref, order_ref, radial_ref, *refs):
    fours, rows, out_ref = refs[:8], refs[8:16], refs[16]
    four_ref, harmonic_ref, block_ref, sems = refs[17:]
    mine = lax.axis_index("shell")
    start = block_start(lengths_ref)
    base, shift = split_start(start)
    for d in range(8):
        four_ref[:, mine ^ d] = fours[d][...].reshape(32, 16, 128)
    lane = lax.broadcasted_iota(jnp.int32, (128, 128), 1)
    slot = lax.broadcasted_iota(jnp.int32, (128, 128), 0)
    degree = base + slot + jnp.where(slot < shift, 128, 0)
    first_half = lane < 64
    tile = lax.broadcasted_iota(jnp.int32, (32, 128), 1) >> 5
    for d in range(8):
        for i in range(4):
            pair = 4 * (mine ^ d) + i
            left = rows[d][2 * i : 2 * i + 2].reshape(256, 128)
            both = jnp.dot(left, four_ref[pair].reshape(128, 128), preferred_element_type=F32)
            value = jnp.where(first_half, both[:128], both[128:])
            order = jnp.where(first_half, order_ref[2 * pair], order_ref[2 * pair + 1])
            value = jnp.where(degree >= order, value, 0.0)
            for u in range(4):
                packed = value[32 * u : 32 * u + 32]
                for j in range(4):
                    if j != u:
                        packed = jnp.where(tile == j, pltpu.roll(value[32 * j : 32 * j + 32], (32 * (j - u)) % 128, 1), packed)
                harmonic_ref[pl.ds(2 * pair + (u & 1) * 64 + (u >> 1), 32, stride=128), :] = packed
    group = lax.broadcasted_iota(jnp.int32, (64, 128), 1) >> 5
    zero = jnp.zeros((64, 128), BF16)
    for g in range(32):
        right = harmonic_ref[128 * g : 128 * g + 128, :].astype(BF16)
        left = jnp.concatenate([jnp.where(group == j, radial_ref[g], zero) for j in range(4)], axis=0)
        result = lax.dot_general(left, right, (((1,), (1,)), ((), ())), preferred_element_type=F32)
        block_ref[:, g] = result.reshape(4, 64, 128).astype(BF16)
        if g % 8 == 7:
            for j in range(4):
                first = g - 7
                sem = sems.at[4 * (g // 8) + j]
                row = (32 * j + first - start) & 127

                @pl.when(row <= 120)
                def _(j=j, first=first, sem=sem, row=row):
                    pltpu.make_async_copy(block_ref.at[j, pl.ds(first, 8)], out_ref.at[pl.ds(row, 8)], sem).start()

                @pl.when(row > 120)
                def _(j=j, first=first, sem=sem, row=row):
                    for i in range(8):
                        pltpu.make_async_copy(block_ref.at[j, first + i], out_ref.at[(row + i) & 127], sem).start()

    for i in range(16):
        pltpu.make_async_copy(block_ref.at[0, pl.ds(0, 8)], out_ref.at[pl.ds(0, 8)], sems.at[i]).wait()


def on_device(density, footprint, cycle_index, order_values, block_lengths, legendre, bessel):
    shape = jax.ShapeDtypeStruct
    rows, nphi = density.shape[1:]
    deg, modes = bessel.shape[1:]
    dma = pltpu.SemaphoreType.DMA

    def swap(x, d):
        return lax.ppermute(x, "shell", [(i, i ^ d) for i in range(8)])

    send, leg_rows = pl.pallas_call(
        front_kernel,
        out_shape=[shape((32, 16 + modes, 128), BF16), shape((8, 128, 128), BF16)],
        in_specs=[HBM_SPEC] * 7,
        out_specs=[HBM_SPEC] * 2,
        scratch_shapes=[
            pltpu.SMEM((32,), jnp.int32),
            pltpu.SMEM((rows,), jnp.int32),
            pltpu.SMEM((64,), jnp.int32),
            pltpu.VMEM((1, rows, nphi), F32),
            pltpu.VMEM((1, rows, nphi), jnp.int32),
            pltpu.VMEM((modes, deg), BF16),
            pltpu.VMEM((8, 128, 128), BF16),
            pltpu.VMEM((8, 128, 128), BF16),
            pltpu.VMEM((32, modes, 128), BF16),
            pltpu.VMEM((32, 16, 128), BF16),
            pltpu.VMEM((8, 128, 128), BF16),
            dma((11,)),
        ],
        compiler_params=params(VMEM_WHOLE),
        cost_estimate=cost(4, 1 << 21),
        name="front",
    )(block_lengths, cycle_index, order_values, density, footprint, jnp.swapaxes(bessel, 1, 2).reshape(modes, deg), legendre)
    recv = lax.all_to_all(send, "radial", split_axis=0, concat_axis=0, tiled=True)

    row_pieces = {0: leg_rows}
    for d in (4, 2, 6):
        row_pieces[d] = swap(leg_rows, d)
    for d in (0, 4, 2, 6):
        row_pieces[d + 1] = swap(row_pieces[d], 1)

    four = pl.pallas_call(
        turn_kernel,
        out_shape=shape((512, 128), BF16),
        in_specs=[VMEM_SPEC],
        out_specs=VMEM_SPEC,
        scratch_shapes=[pltpu.VMEM((512, 128), F32), pltpu.VMEM((512, 128), F32)],
        compiler_params=params(),
        cost_estimate=cost(1, 1 << 19),
        name="turn",
    )(recv)

    radial = pl.pallas_call(
        radial_kernel,
        out_shape=shape((32, modes, 128), BF16),
        in_specs=[SMEM_SPEC, VMEM_SPEC],
        out_specs=VMEM_SPEC,
        scratch_shapes=[pltpu.VMEM((32 * modes, 128), F32), pltpu.VMEM((32 * modes, 128), F32)],
        compiler_params=params(),
        cost_estimate=cost(3, 1 << 20),
        name="radial_rows",
    )(block_lengths, recv)

    pieces = {0: four}
    for d in (2, 6, 4):
        pieces[d] = swap(four, d)
    own, radial = lax.optimization_barrier((four, radial))
    pieces[1] = swap(own, 1)
    for d in (2, 6, 4):
        pieces[d + 1] = swap(pieces[d], 1)

    return pl.pallas_call(
        final_kernel,
        out_shape=shape((128, modes, 128), BF16),
        in_specs=[SMEM_SPEC] * 2 + [VMEM_SPEC] * 17,
        out_specs=HBM_SPEC,
        scratch_shapes=[
            pltpu.VMEM((32, 8, 16, 128), BF16),
            pltpu.VMEM((32 * 128, 128), F32),
            pltpu.VMEM((4, 32, modes, 128), BF16),
            dma((16,)),
        ],
        compiler_params=params(),
        cost_estimate=cost(5, 1 << 22),
        name="finish",
    )(block_lengths, order_values, radial, *[pieces[d] for d in range(8)], *[row_pieces[d] for d in range(8)])


def solution(mesh):
    return jax.shard_map(
        on_device,
        mesh=mesh,
        in_specs=(
            P("radial", "shell", None),
            P("radial", "shell", None),
            P("shell"),
            P(),
            P(),
            P("shell", None, None),
            P("radial", None, "shell"),
        ),
        out_specs=P("radial", "shell", None),
        check_vma=False,
    )
```

```python
import math

import jax
import jax.numpy as jnp
from jax import lax
from jax.experimental import pallas as pl
from jax.experimental.pallas import tpu as pltpu
from jax.sharding import PartitionSpec as P

NSIDE = 1024
F32 = jnp.float32
BF16 = jnp.bfloat16
VMEM_LIMIT = 16 * 1024 * 1024
VMEM_WHOLE = 64 * 1024 * 1024

VMEM_SPEC = pl.BlockSpec(memory_space=pltpu.VMEM)
HBM_SPEC = pl.BlockSpec(memory_space=pltpu.HBM)


def params(limit=VMEM_LIMIT):
    return pltpu.CompilerParams(vmem_limit_bytes=limit)


def cost(microseconds, transferred):
    return pl.CostEstimate(flops=microseconds * 500_000_000, bytes_accessed=transferred, transcendentals=0)


def split_start(start):
    base = pl.multiple_of((start >> 7) << 7, 128)
    return base, start - base


def cos_sin(turns):
    quarter = (turns + 1024) >> 11
    x = (turns - (quarter << 11)).astype(F32) * (math.pi / 4096)
    z = x * x
    s = x + x * z * (-1.6666654611e-1 + z * (8.3321608736e-3 + z * -1.9515295891e-4))
    c = 1.0 - 0.5 * z + z * z * (4.166664568298827e-2 + z * (-1.388731625493765e-3 + z * 2.443315711809948e-5))
    odd = (quarter & 1) == 1
    even_sign = jnp.where((quarter & 2) == 2, -1.0, 1.0)
    cos = jnp.where(odd, -s, c) * even_sign
    sin = jnp.where(odd, c, s) * even_sign
    return cos, sin


def front_kernel(
    lengths_hbm, cycle_hbm, order_hbm, density_hbm, footprint_hbm, bessel_hbm, legendre_hbm, send_hbm, rows_hbm, info_hbm,
    lengths_ref, cycle_ref, order_ref, density_ref, footprint_ref, bessel_ref, low_ref, high_ref,
    block_ref, tile_ref, rows_ref, info_ref, sems,
):
    _, rows, nphi = density_ref.shape
    modes, deg = bessel_ref.shape
    inputs = [
        (lengths_hbm, lengths_ref),
        (bessel_hbm, bessel_ref),
        (order_hbm, order_ref),
        (density_hbm, density_ref),
        (footprint_hbm, footprint_ref),
        (cycle_hbm, cycle_ref),
    ]
    copies = [pltpu.make_async_copy(source, target, sems.at[i]) for i, (source, target) in enumerate(inputs)]
    for copy in copies:
        copy.start()
    copies[0].wait()
    first = block_start(lengths_ref)
    base, shift = split_start(first)
    after = pl.multiple_of(jnp.minimum(base + 128, deg - 128), 128)
    windows = [
        pltpu.make_async_copy(legendre_hbm.at[:, pl.ds(base, 128), :], low_ref, sems.at[6]),
        pltpu.make_async_copy(legendre_hbm.at[:, pl.ds(after, 128), :], high_ref, sems.at[7]),
    ]
    for copy in windows:
        copy.start()
    copies[1].wait()
    lane = lax.broadcasted_iota(jnp.int32, (modes, 128), 1)
    tile = lax.broadcasted_iota(jnp.int32, (16, 128), 1) >> 5

    def step(k, start):
        base, shift = split_start(start)
        after = pl.multiple_of(jnp.minimum(base + 128, deg - 128), 128)
        block = jnp.where(lane >= shift, bessel_ref[:, pl.ds(base, 128)], bessel_ref[:, pl.ds(after, 128)])
        for j in range(4):
            row = block[16 * j : 16 * j + 16]
            for i in range(4):
                if i != j:
                    row = jnp.where(tile == i, pltpu.roll(block[16 * i : 16 * i + 16], (32 * (i - j)) % 128, 1), row)
            block_ref[k, 16 * j : 16 * j + 16, :] = row
        return start + lengths_ref[k]

    lax.fori_loop(0, block_ref.shape[0], step, jnp.int32(0), unroll=4)
    outputs = [pltpu.make_async_copy(block_ref, send_hbm.at[:, pl.ds(16, modes), :], sems.at[8])]
    outputs[0].start()

    for copy in windows:
        copy.wait()
    slot = lax.broadcasted_iota(jnp.int32, (128, 128), 0)
    for q in range(rows_ref.shape[0]):
        rows_ref[q] = jnp.where(slot >= shift, low_ref[q], high_ref[q])
    outputs.append(pltpu.make_async_copy(rows_ref, rows_hbm, sems.at[9]))
    outputs[1].start()

    for copy in copies[2:]:
        copy.wait()
    lane = lax.broadcasted_iota(jnp.int32, (1, 128), 1)
    part = (lane >> 5) & 1
    order_slot = 2 * (lane & 31) + (lane >> 6)
    order = jnp.zeros((1, 128), jnp.int32)
    for q in range(64):
        order = jnp.where(order_slot == q, order_ref[q], order)
    sixty_four = lax.broadcasted_iota(jnp.int32, (64, 128), 0)
    pa, qa = cos_sin((sixty_four * 128 * order + 2048 * part) & 8191)
    qa = -qa
    cb, sb = cos_sin((sixty_four * 2 * order) & 8191)
    info_ref[32:33] = jnp.full((1, 128), first, jnp.int32)
    info_ref[33:34] = jnp.full((1, 128), lengths_ref[lax.axis_index("radial")], jnp.int32)
    for i in range(32):
        info_ref[i : i + 1] = jnp.where(lane < 64, order_ref[2 * i], order_ref[2 * i + 1])
    outputs.append(pltpu.make_async_copy(info_ref, info_hbm, sems.at[11]))
    outputs[2].start()
    total = jnp.zeros((2 * rows, 256), F32)
    for chunk in range(nphi // 256):
        tables = []
        for a in range(4 * chunk, 4 * chunk + 4):
            tables.append(pa[a : a + 1] * cb + qa[a : a + 1] * sb)
        table = jnp.concatenate(tables, axis=0)
        high = table.astype(BF16)
        low = (table - high.astype(F32)).astype(BF16)
        cut = slice(256 * chunk, 256 * chunk + 256)
        pixels = density_ref[0, :, cut] * footprint_ref[0, :, cut].astype(F32)
        p_high = pixels.astype(BF16)
        p_low = (pixels - p_high.astype(F32)).astype(BF16)
        total = total + jnp.dot(
            jnp.concatenate([p_high, p_low], axis=0),
            jnp.concatenate([high, low], axis=1),
            preferred_element_type=F32,
        )
    x = total[:rows, :128] + (total[:rows, 128:] + total[rows:, :128])
    row = lax.broadcasted_iota(jnp.int32, (rows, 128), 0)
    cycle = jnp.zeros((rows, 128), jnp.int32)
    for r in range(rows):
        cycle = jnp.where(row == r, cycle_ref[r], cycle)
    parity = (cycle - (NSIDE - 1)) & 1
    cos_t, sin_t = cos_sin((order * (2 - parity)) & 8191)
    other = jnp.where(part == 0, pltpu.roll(x, 96, 1), -pltpu.roll(x, 32, 1))
    four = (x * cos_t + other * sin_t).astype(BF16)
    tile_ref[...] = jnp.broadcast_to(four[None], tile_ref.shape)
    outputs.append(pltpu.make_async_copy(tile_ref, send_hbm.at[:, pl.ds(0, 16), :], sems.at[10]))
    outputs[3].start()
    for copy in outputs:
        copy.wait()


def turn_kernel(recv_ref, out_ref, wide_ref, turned_ref):
    for s in range(32):
        wide_ref[24 * s : 24 * s + 16, :] = recv_ref[s, :16].astype(F32)
    tile = lax.broadcasted_iota(jnp.int32, (32, 128), 1) >> 5
    for a in range(4):
        x = [wide_ref[pl.ds(4 * a + b, 32, stride=24), :] for b in range(4)]
        pieces = []
        for u in range(4):
            piece = x[u]
            for b in range(4):
                if b != u:
                    piece = jnp.where(tile == b, pltpu.roll(x[b], (32 * (b - u)) % 128, 1), piece)
            pieces.append(piece)
        turned = jnp.transpose(jnp.concatenate(pieces, axis=0))
        for b in range(4):
            turned_ref[pl.ds(4 * a + b, 32, stride=24), :] = turned[32 * b : 32 * b + 32]
    for i in range(32):
        out_ref[16 * i : 16 * i + 16] = turned_ref[24 * i : 24 * i + 16, :].astype(BF16)


def block_start(lengths_ref):
    return lax.fori_loop(0, lax.axis_index("radial"), lambda k, total: total + lengths_ref[k], jnp.int32(0))


def radial_kernel(info_ref, recv_ref, out_ref, wide_ref, turned_ref):
    for s in range(32):
        wide_ref[72 * s : 72 * s + 64, :] = recv_ref[s, 16:].astype(F32)
    lane = lax.broadcasted_iota(jnp.int32, (128, 128), 1)
    row = lax.broadcasted_iota(jnp.int32, (128, 128), 0)
    slot = 32 * (row >> 5) + (lane & 31)
    keep = ((slot - info_ref[32:33]) & 127) < info_ref[33:34]

    def step(a, carry):
        x = jnp.concatenate([wide_ref[pl.ds(16 * j + a, 32, stride=72), :] for j in range(4)], axis=0)
        turned = jnp.transpose(jnp.where(keep, x, 0.0))
        for m in range(4):
            turned_ref[pl.ds(16 * m + a, 32, stride=72), :] = turned[32 * m : 32 * m + 32]
        return carry

    lax.fori_loop(0, 16, step, 0, unroll=4)
    for g in range(32):
        out_ref[g] = turned_ref[72 * g : 72 * g + 64, :].astype(BF16)


def final_kernel(info_ref, radial_ref, *refs):
    fours, rows, out_ref = refs[:8], refs[8:16], refs[16]
    four_ref, harmonic_ref, block_ref, sems = refs[17:]
    mine = lax.axis_index("shell")
    start = jnp.max(info_ref[32:33].astype(F32)).astype(jnp.int32)
    shift = info_ref[32:33] & 127
    base = info_ref[32:33] - shift
    for d in range(8):
        four_ref[:, mine ^ d] = fours[d][...].reshape(32, 16, 128)
    lane = lax.broadcasted_iota(jnp.int32, (128, 128), 1)
    slot = lax.broadcasted_iota(jnp.int32, (128, 128), 0)
    degree = base + slot + jnp.where(slot < shift, 128, 0)
    first_half = lane < 64
    tile = lax.broadcasted_iota(jnp.int32, (32, 128), 1) >> 5
    for d in range(8):
        for i in range(4):
            pair = 4 * (mine ^ d) + i
            left = rows[d][2 * i : 2 * i + 2].reshape(256, 128)
            both = jnp.dot(left, four_ref[pair].reshape(128, 128), preferred_element_type=F32)
            value = jnp.where(first_half, both[:128], both[128:])
            value = jnp.where(degree >= info_ref[pl.ds(pair, 1), :], value, 0.0)
            for u in range(4):
                packed = value[32 * u : 32 * u + 32]
                for j in range(4):
                    if j != u:
                        packed = jnp.where(tile == j, pltpu.roll(value[32 * j : 32 * j + 32], (32 * (j - u)) % 128, 1), packed)
                harmonic_ref[pl.ds(2 * pair + (u & 1) * 64 + (u >> 1), 32, stride=136), :] = packed
    group = lax.broadcasted_iota(jnp.int32, (64, 128), 1) >> 5
    zero = jnp.zeros((64, 128), BF16)
    for g in range(32):
        right = harmonic_ref[136 * g : 136 * g + 128, :].astype(BF16)
        left = jnp.concatenate([jnp.where(group == j, radial_ref[g], zero) for j in range(4)], axis=0)
        result = lax.dot_general(left, right, (((1,), (1,)), ((), ())), preferred_element_type=F32)
        block_ref[:, g] = result.reshape(4, 64, 128).astype(BF16)
        if g % 8 == 7:
            for j in range(4):
                first = g - 7
                sem = sems.at[4 * (g // 8) + j]
                row = (32 * j + first - start) & 127

                @pl.when(row <= 120)
                def _(j=j, first=first, sem=sem, row=row):
                    pltpu.make_async_copy(block_ref.at[j, pl.ds(first, 8)], out_ref.at[pl.ds(row, 8)], sem).start()

                @pl.when(row > 120)
                def _(j=j, first=first, sem=sem, row=row):
                    for i in range(8):
                        pltpu.make_async_copy(block_ref.at[j, first + i], out_ref.at[(row + i) & 127], sem).start()

    for i in range(16):
        pltpu.make_async_copy(block_ref.at[0, pl.ds(0, 8)], out_ref.at[pl.ds(0, 8)], sems.at[i]).wait()


def on_device(density, footprint, cycle_index, order_values, block_lengths, legendre, bessel):
    shape = jax.ShapeDtypeStruct
    rows, nphi = density.shape[1:]
    deg, modes = bessel.shape[1:]
    dma = pltpu.SemaphoreType.DMA

    def swap(x, d):
        return lax.ppermute(x, "shell", [(i, i ^ d) for i in range(8)])

    send, leg_rows, info = pl.pallas_call(
        front_kernel,
        out_shape=[shape((32, 16 + modes, 128), BF16), shape((8, 128, 128), BF16), shape((40, 128), jnp.int32)],
        in_specs=[HBM_SPEC] * 7,
        out_specs=[HBM_SPEC] * 3,
        scratch_shapes=[
            pltpu.SMEM((32,), jnp.int32),
            pltpu.SMEM((rows,), jnp.int32),
            pltpu.SMEM((64,), jnp.int32),
            pltpu.VMEM((1, rows, nphi), F32),
            pltpu.VMEM((1, rows, nphi), jnp.int32),
            pltpu.VMEM((modes, deg), BF16),
            pltpu.VMEM((8, 128, 128), BF16),
            pltpu.VMEM((8, 128, 128), BF16),
            pltpu.VMEM((32, modes, 128), BF16),
            pltpu.VMEM((32, 16, 128), BF16),
            pltpu.VMEM((8, 128, 128), BF16),
            pltpu.VMEM((40, 128), jnp.int32),
            dma((12,)),
        ],
        compiler_params=params(VMEM_WHOLE),
        cost_estimate=cost(4, 1 << 21),
        name="front",
    )(block_lengths, cycle_index, order_values, density, footprint, jnp.swapaxes(bessel, 1, 2).reshape(modes, deg), legendre)
    recv = lax.all_to_all(send, "radial", split_axis=0, concat_axis=0, tiled=True)

    row_pieces = {0: leg_rows, 1: swap(leg_rows, 1)}
    for d in (4, 2, 6):
        row_pieces[d] = swap(leg_rows, d)

    four = pl.pallas_call(
        turn_kernel,
        out_shape=shape((512, 128), BF16),
        in_specs=[VMEM_SPEC],
        out_specs=VMEM_SPEC,
        scratch_shapes=[pltpu.VMEM((32 * 24, 128), F32)] * 2,
        compiler_params=params(),
        cost_estimate=cost(1, 1 << 19),
        name="turn",
    )(recv)

    radial = pl.pallas_call(
        radial_kernel,
        out_shape=shape((32, modes, 128), BF16),
        in_specs=[VMEM_SPEC] * 2,
        out_specs=VMEM_SPEC,
        scratch_shapes=[pltpu.VMEM((32 * 72, 128), F32)] * 2,
        compiler_params=params(),
        cost_estimate=cost(3, 1 << 20),
        name="radial_rows",
    )(info, recv)

    pieces = {0: four}
    for d in (2, 6, 4):
        pieces[d] = swap(four, d)
    own, radial, *moved = lax.optimization_barrier((four, radial, *[row_pieces[d] for d in (4, 2, 6)]))
    pieces[1] = swap(own, 1)
    for d, piece in zip((4, 2, 6), moved):
        row_pieces[d] = piece
        row_pieces[d + 1] = swap(piece, 1)
    for d in (2, 6, 4):
        pieces[d + 1] = swap(pieces[d], 1)

    return pl.pallas_call(
        final_kernel,
        out_shape=shape((128, modes, 128), BF16),
        in_specs=[VMEM_SPEC] * 18,
        out_specs=HBM_SPEC,
        scratch_shapes=[
            pltpu.VMEM((32, 8, 16, 128), BF16),
            pltpu.VMEM((32 * 136, 128), F32),
            pltpu.VMEM((4, 32, modes, 128), BF16),
            dma((16,)),
        ],
        compiler_params=params(),
        cost_estimate=cost(5, 1 << 22),
        name="finish",
    )(info, radial, *[pieces[d] for d in range(8)], *[row_pieces[d] for d in range(8)])


def solution(mesh):
    return jax.shard_map(
        on_device,
        mesh=mesh,
        in_specs=(
            P("radial", "shell", None),
            P("radial", "shell", None),
            P("shell"),
            P(),
            P(),
            P("shell", None, None),
            P("radial", None, "shell"),
        ),
        out_specs=P("radial", "shell", None),
        check_vma=False,
    )
```

```python
import math

import jax
import jax.numpy as jnp
from jax import lax
from jax.experimental import pallas as pl
from jax.experimental.pallas import tpu as pltpu
from jax.sharding import PartitionSpec as P

NSIDE = 1024
F32 = jnp.float32
BF16 = jnp.bfloat16
VMEM_LIMIT = 16 * 1024 * 1024
VMEM_WHOLE = 64 * 1024 * 1024

VMEM_SPEC = pl.BlockSpec(memory_space=pltpu.VMEM)
HBM_SPEC = pl.BlockSpec(memory_space=pltpu.HBM)


def params(limit=VMEM_LIMIT):
    return pltpu.CompilerParams(vmem_limit_bytes=limit)


def cost(microseconds, transferred):
    return pl.CostEstimate(flops=microseconds * 500_000_000, bytes_accessed=transferred, transcendentals=0)


def split_start(start):
    base = pl.multiple_of((start >> 7) << 7, 128)
    return base, start - base


def swap_tiles(blocks, width):
    tile = lax.broadcasted_iota(jnp.int32, (width, 128), 1) >> 5
    odd, upper = (tile & 1) == 1, tile >= 2
    middle = []
    for p in (0, 2):
        middle.append(jnp.where(odd, pltpu.roll(blocks[p + 1], 32, 1), blocks[p]))
        middle.append(jnp.where(odd, blocks[p + 1], pltpu.roll(blocks[p], 96, 1)))
    low = [jnp.where(upper, pltpu.roll(middle[p + 2], 64, 1), middle[p]) for p in (0, 1)]
    high = [jnp.where(upper, middle[p + 2], pltpu.roll(middle[p], 64, 1)) for p in (0, 1)]
    return low + high


def cos_sin(turns):
    quarter = (turns + 1024) >> 11
    x = (turns - (quarter << 11)).astype(F32) * (math.pi / 4096)
    z = x * x
    s = x + x * z * (-1.6666654611e-1 + z * (8.3321608736e-3 + z * -1.9515295891e-4))
    c = 1.0 - 0.5 * z + z * z * (4.166664568298827e-2 + z * (-1.388731625493765e-3 + z * 2.443315711809948e-5))
    odd = (quarter & 1) == 1
    even_sign = jnp.where((quarter & 2) == 2, -1.0, 1.0)
    cos = jnp.where(odd, -s, c) * even_sign
    sin = jnp.where(odd, c, s) * even_sign
    return cos, sin


def front_kernel(
    lengths_hbm, cycle_hbm, order_hbm, density_hbm, footprint_hbm, bessel_hbm, legendre_hbm, send_hbm, rows_hbm, info_hbm,
    lengths_ref, cycle_ref, order_ref, density_ref, footprint_ref, bessel_ref, low_ref, high_ref,
    block_ref, tile_ref, rows_ref, info_ref, sems,
):
    _, rows, nphi = density_ref.shape
    modes, deg = bessel_ref.shape
    inputs = [
        (lengths_hbm, lengths_ref),
        (bessel_hbm, bessel_ref),
        (order_hbm, order_ref),
        (density_hbm, density_ref),
        (footprint_hbm, footprint_ref),
        (cycle_hbm, cycle_ref),
    ]
    copies = [pltpu.make_async_copy(source, target, sems.at[i]) for i, (source, target) in enumerate(inputs)]
    for copy in copies:
        copy.start()
    copies[0].wait()
    first = block_start(lengths_ref)
    base, shift = split_start(first)
    after = pl.multiple_of(jnp.minimum(base + 128, deg - 128), 128)
    windows = [
        pltpu.make_async_copy(legendre_hbm.at[:, pl.ds(base, 128), :], low_ref, sems.at[6]),
        pltpu.make_async_copy(legendre_hbm.at[:, pl.ds(after, 128), :], high_ref, sems.at[7]),
    ]
    for copy in windows:
        copy.start()
    copies[1].wait()
    lane_in_block = lax.broadcasted_iota(jnp.int32, (modes, 128), 1)

    def step(k, start):
        base, shift = split_start(start)
        after = pl.multiple_of(jnp.minimum(base + 128, deg - 128), 128)
        block = jnp.where(lane_in_block >= shift, bessel_ref[:, pl.ds(base, 128)], bessel_ref[:, pl.ds(after, 128)])
        for j, row in enumerate(swap_tiles([block[16 * i : 16 * i + 16] for i in range(4)], 16)):
            block_ref[k, 16 * j : 16 * j + 16, :] = row
        return start + lengths_ref[k]

    lax.fori_loop(0, block_ref.shape[0], step, jnp.int32(0), unroll=16)
    outputs = [pltpu.make_async_copy(block_ref, send_hbm.at[:, pl.ds(16, modes), :], sems.at[8])]
    outputs[0].start()

    for copy in windows:
        copy.wait()
    slot = lax.broadcasted_iota(jnp.int32, (128, 128), 0)
    for q in range(rows_ref.shape[0]):
        rows_ref[q] = jnp.where(slot >= shift, low_ref[q], high_ref[q])
    outputs.append(pltpu.make_async_copy(rows_ref, rows_hbm, sems.at[9]))
    outputs[1].start()

    for copy in copies[2:]:
        copy.wait()
    lane = lax.broadcasted_iota(jnp.int32, (1, 128), 1)
    part = (lane >> 5) & 1
    order_slot = 2 * (lane & 31) + (lane >> 6)
    order = jnp.zeros((1, 128), jnp.int32)
    for q in range(64):
        order = jnp.where(order_slot == q, order_ref[q], order)
    sixty_four = lax.broadcasted_iota(jnp.int32, (64, 128), 0)
    pa, qa = cos_sin((sixty_four * 128 * order + 2048 * part) & 8191)
    qa = -qa
    cb, sb = cos_sin((sixty_four * 2 * order) & 8191)
    info_ref[32:33] = jnp.full((1, 128), first, jnp.int32)
    info_ref[33:34] = jnp.full((1, 128), lengths_ref[lax.axis_index("radial")], jnp.int32)
    for i in range(32):
        info_ref[i : i + 1] = jnp.where(lane < 64, order_ref[2 * i], order_ref[2 * i + 1])
    outputs.append(pltpu.make_async_copy(info_ref, info_hbm, sems.at[11]))
    outputs[2].start()
    total = jnp.zeros((2 * rows, 256), F32)
    for chunk in range(nphi // 256):
        tables = []
        for a in range(4 * chunk, 4 * chunk + 4):
            tables.append(pa[a : a + 1] * cb + qa[a : a + 1] * sb)
        table = jnp.concatenate(tables, axis=0)
        high = table.astype(BF16)
        low = (table - high.astype(F32)).astype(BF16)
        cut = slice(256 * chunk, 256 * chunk + 256)
        pixels = density_ref[0, :, cut] * footprint_ref[0, :, cut].astype(F32)
        p_high = pixels.astype(BF16)
        p_low = (pixels - p_high.astype(F32)).astype(BF16)
        total = total + jnp.dot(
            jnp.concatenate([p_high, p_low], axis=0),
            jnp.concatenate([high, low], axis=1),
            preferred_element_type=F32,
        )
    x = total[:rows, :128] + (total[:rows, 128:] + total[rows:, :128])
    row = lax.broadcasted_iota(jnp.int32, (rows, 128), 0)
    cycle = jnp.zeros((rows, 128), jnp.int32)
    for r in range(rows):
        cycle = jnp.where(row == r, cycle_ref[r], cycle)
    parity = (cycle - (NSIDE - 1)) & 1
    cos_t, sin_t = cos_sin((order * (2 - parity)) & 8191)
    other = jnp.where(part == 0, pltpu.roll(x, 96, 1), -pltpu.roll(x, 32, 1))
    four = (x * cos_t + other * sin_t).astype(BF16)
    tile_ref[...] = jnp.broadcast_to(four[None], tile_ref.shape)
    outputs.append(pltpu.make_async_copy(tile_ref, send_hbm.at[:, pl.ds(0, 16), :], sems.at[10]))
    outputs[3].start()
    for copy in outputs:
        copy.wait()


def turn_kernel(recv_ref, out_ref, wide_ref, turned_ref):
    for s in range(32):
        wide_ref[24 * s : 24 * s + 16, :] = recv_ref[s, :16].astype(F32)
    for a in range(4):
        pieces = swap_tiles([wide_ref[pl.ds(4 * a + b, 32, stride=24), :] for b in range(4)], 32)
        turned = jnp.transpose(jnp.concatenate(pieces, axis=0))
        for b in range(4):
            turned_ref[pl.ds(4 * a + b, 32, stride=24), :] = turned[32 * b : 32 * b + 32]
    for i in range(32):
        out_ref[16 * i : 16 * i + 16] = turned_ref[24 * i : 24 * i + 16, :].astype(BF16)


def block_start(lengths_ref):
    return lax.fori_loop(0, lax.axis_index("radial"), lambda k, total: total + lengths_ref[k], jnp.int32(0))


def radial_kernel(info_ref, recv_ref, out_ref, wide_ref, turned_ref):
    for s in range(32):
        wide_ref[72 * s : 72 * s + 64, :] = recv_ref[s, 16:].astype(F32)
    lane = lax.broadcasted_iota(jnp.int32, (128, 128), 1)
    row = lax.broadcasted_iota(jnp.int32, (128, 128), 0)
    slot = 32 * (row >> 5) + (lane & 31)
    keep = ((slot - info_ref[32:33]) & 127) < info_ref[33:34]

    def step(a, carry):
        x = jnp.concatenate([wide_ref[pl.ds(16 * j + a, 32, stride=72), :] for j in range(4)], axis=0)
        turned = jnp.transpose(jnp.where(keep, x, 0.0))
        for m in range(4):
            turned_ref[pl.ds(16 * m + a, 32, stride=72), :] = turned[32 * m : 32 * m + 32]
        return carry

    lax.fori_loop(0, 16, step, 0, unroll=4)
    for g in range(32):
        out_ref[g] = turned_ref[72 * g : 72 * g + 64, :].astype(BF16)


def final_kernel(info_ref, radial_ref, *refs):
    fours, rows, out_ref = refs[:8], refs[8:16], refs[16]
    four_ref, harmonic_ref, block_ref, sems = refs[17:]
    mine = lax.axis_index("shell")
    start = jnp.max(info_ref[32:33].astype(F32)).astype(jnp.int32)
    shift = info_ref[32:33] & 127
    base = info_ref[32:33] - shift
    for d in range(8):
        four_ref[:, mine ^ d] = fours[d][...].reshape(32, 16, 128)
    lane = lax.broadcasted_iota(jnp.int32, (128, 128), 1)
    slot = lax.broadcasted_iota(jnp.int32, (128, 128), 0)
    degree = base + slot + jnp.where(slot < shift, 128, 0)
    first_half = lane < 64
    for d in range(8):
        for i in range(4):
            pair = 4 * (mine ^ d) + i
            left = rows[d][2 * i : 2 * i + 2].reshape(256, 128)
            both = jnp.dot(left, four_ref[pair].reshape(128, 128), preferred_element_type=F32)
            value = jnp.where(first_half, both[:128], both[128:])
            value = jnp.where(degree >= info_ref[pl.ds(pair, 1), :], value, 0.0).astype(BF16)
            for u, packed in enumerate(swap_tiles([value[32 * j : 32 * j + 32] for j in range(4)], 32)):
                harmonic_ref[pl.ds(2 * pair + (u & 1) * 64 + (u >> 1), 32, stride=136), :] = packed.astype(F32)
    group = lax.broadcasted_iota(jnp.int32, (64, 128), 1) >> 5
    zero = jnp.zeros((64, 128), BF16)
    for g in range(32):
        right = harmonic_ref[136 * g : 136 * g + 128, :].astype(BF16)
        left = jnp.concatenate([jnp.where(group == j, radial_ref[g], zero) for j in range(4)], axis=0)
        result = lax.dot_general(left, right, (((1,), (1,)), ((), ())), preferred_element_type=F32)
        block_ref[:, g] = result.reshape(4, 64, 128).astype(BF16)
        if g % 8 == 7:
            for j in range(4):
                first = g - 7
                sem = sems.at[4 * (g // 8) + j]
                row = (32 * j + first - start) & 127

                @pl.when(row <= 120)
                def _(j=j, first=first, sem=sem, row=row):
                    pltpu.make_async_copy(block_ref.at[j, pl.ds(first, 8)], out_ref.at[pl.ds(row, 8)], sem).start()

                @pl.when(row > 120)
                def _(j=j, first=first, sem=sem, row=row):
                    for i in range(8):
                        pltpu.make_async_copy(block_ref.at[j, first + i], out_ref.at[(row + i) & 127], sem).start()

    for i in range(16):
        pltpu.make_async_copy(block_ref.at[0, pl.ds(0, 8)], out_ref.at[pl.ds(0, 8)], sems.at[i]).wait()


def on_device(density, footprint, cycle_index, order_values, block_lengths, legendre, bessel):
    shape = jax.ShapeDtypeStruct
    rows, nphi = density.shape[1:]
    deg, modes = bessel.shape[1:]
    dma = pltpu.SemaphoreType.DMA

    def swap(x, d):
        return lax.ppermute(x, "shell", [(i, i ^ d) for i in range(8)])

    send, leg_rows, info = pl.pallas_call(
        front_kernel,
        out_shape=[shape((32, 16 + modes, 128), BF16), shape((8, 128, 128), BF16), shape((40, 128), jnp.int32)],
        in_specs=[HBM_SPEC] * 7,
        out_specs=[HBM_SPEC] * 3,
        scratch_shapes=[
            pltpu.SMEM((32,), jnp.int32),
            pltpu.SMEM((rows,), jnp.int32),
            pltpu.SMEM((64,), jnp.int32),
            pltpu.VMEM((1, rows, nphi), F32),
            pltpu.VMEM((1, rows, nphi), jnp.int32),
            pltpu.VMEM((modes, deg), BF16),
            pltpu.VMEM((8, 128, 128), BF16),
            pltpu.VMEM((8, 128, 128), BF16),
            pltpu.VMEM((32, modes, 128), BF16),
            pltpu.VMEM((32, 16, 128), BF16),
            pltpu.VMEM((8, 128, 128), BF16),
            pltpu.VMEM((40, 128), jnp.int32),
            dma((12,)),
        ],
        compiler_params=params(VMEM_WHOLE),
        cost_estimate=cost(4, 1 << 21),
        name="front",
    )(block_lengths, cycle_index, order_values, density, footprint, jnp.swapaxes(bessel, 1, 2).reshape(modes, deg), legendre)
    recv = lax.all_to_all(send, "radial", split_axis=0, concat_axis=0, tiled=True)

    row_pieces = {0: leg_rows, 1: swap(leg_rows, 1)}
    for d in (4, 2, 6):
        row_pieces[d] = swap(leg_rows, d)

    four = pl.pallas_call(
        turn_kernel,
        out_shape=shape((512, 128), BF16),
        in_specs=[VMEM_SPEC],
        out_specs=VMEM_SPEC,
        scratch_shapes=[pltpu.VMEM((32 * 24, 128), F32)] * 2,
        compiler_params=params(),
        cost_estimate=cost(1, 1 << 19),
        name="turn",
    )(recv)

    radial = pl.pallas_call(
        radial_kernel,
        out_shape=shape((32, modes, 128), BF16),
        in_specs=[VMEM_SPEC] * 2,
        out_specs=VMEM_SPEC,
        scratch_shapes=[pltpu.VMEM((32 * 72, 128), F32)] * 2,
        compiler_params=params(),
        cost_estimate=cost(3, 1 << 20),
        name="radial_rows",
    )(info, recv)

    pieces = {0: four}
    for d in (2, 6, 4):
        pieces[d] = swap(four, d)
    own, radial, *moved = lax.optimization_barrier((four, radial, *[row_pieces[d] for d in (4, 2, 6)]))
    pieces[1] = swap(own, 1)
    for d, piece in zip((4, 2, 6), moved):
        row_pieces[d] = piece
        row_pieces[d + 1] = swap(piece, 1)
    for d in (2, 6, 4):
        pieces[d + 1] = swap(pieces[d], 1)

    return pl.pallas_call(
        final_kernel,
        out_shape=shape((128, modes, 128), BF16),
        in_specs=[VMEM_SPEC] * 18,
        out_specs=HBM_SPEC,
        scratch_shapes=[
            pltpu.VMEM((32, 8, 16, 128), BF16),
            pltpu.VMEM((32 * 136, 128), F32),
            pltpu.VMEM((4, 32, modes, 128), BF16),
            dma((16,)),
        ],
        compiler_params=params(),
        cost_estimate=cost(5, 1 << 22),
        name="finish",
    )(info, radial, *[pieces[d] for d in range(8)], *[row_pieces[d] for d in range(8)])


def solution(mesh):
    return jax.shard_map(
        on_device,
        mesh=mesh,
        in_specs=(
            P("radial", "shell", None),
            P("radial", "shell", None),
            P("shell"),
            P(),
            P(),
            P("shell", None, None),
            P("radial", None, "shell"),
        ),
        out_specs=P("radial", "shell", None),
        check_vma=False,
    )
```

```python
import math

import jax
import jax.numpy as jnp
from jax import lax
from jax.experimental import pallas as pl
from jax.experimental.pallas import tpu as pltpu
from jax.sharding import PartitionSpec as P

NSIDE = 1024
F32 = jnp.float32
BF16 = jnp.bfloat16
VMEM_LIMIT = 16 * 1024 * 1024
VMEM_WHOLE = 64 * 1024 * 1024

VMEM_SPEC = pl.BlockSpec(memory_space=pltpu.VMEM)
HBM_SPEC = pl.BlockSpec(memory_space=pltpu.HBM)


def params(limit=VMEM_LIMIT):
    return pltpu.CompilerParams(vmem_limit_bytes=limit)


def cost(microseconds, transferred):
    return pl.CostEstimate(flops=microseconds * 500_000_000, bytes_accessed=transferred, transcendentals=0)


def split_start(start):
    base = pl.multiple_of((start >> 7) << 7, 128)
    return base, start - base


def swap_tiles(blocks, width):
    tile = lax.broadcasted_iota(jnp.int32, (width, 128), 1) >> 5
    odd, upper = (tile & 1) == 1, tile >= 2
    middle = []
    for p in (0, 2):
        middle.append(jnp.where(odd, pltpu.roll(blocks[p + 1], 32, 1), blocks[p]))
        middle.append(jnp.where(odd, blocks[p + 1], pltpu.roll(blocks[p], 96, 1)))
    low = [jnp.where(upper, pltpu.roll(middle[p + 2], 64, 1), middle[p]) for p in (0, 1)]
    high = [jnp.where(upper, middle[p + 2], pltpu.roll(middle[p], 64, 1)) for p in (0, 1)]
    return low + high


def cos_sin(turns):
    quarter = (turns + 1024) >> 11
    x = (turns - (quarter << 11)).astype(F32) * (math.pi / 4096)
    z = x * x
    s = x + x * z * (-1.6666654611e-1 + z * (8.3321608736e-3 + z * -1.9515295891e-4))
    c = 1.0 - 0.5 * z + z * z * (4.166664568298827e-2 + z * (-1.388731625493765e-3 + z * 2.443315711809948e-5))
    odd = (quarter & 1) == 1
    even_sign = jnp.where((quarter & 2) == 2, -1.0, 1.0)
    cos = jnp.where(odd, -s, c) * even_sign
    sin = jnp.where(odd, c, s) * even_sign
    return cos, sin


def front_kernel(
    lengths_hbm, cycle_hbm, order_hbm, density_hbm, footprint_hbm, bessel_hbm, legendre_hbm, send_hbm, rows_hbm, info_hbm,
    lengths_ref, cycle_ref, order_ref, density_ref, footprint_ref, bessel_ref, low_ref, high_ref,
    block_ref, tile_ref, rows_ref, info_ref, sems,
):
    _, rows, nphi = density_ref.shape
    modes, deg = bessel_ref.shape
    inputs = [
        (lengths_hbm, lengths_ref),
        (bessel_hbm, bessel_ref),
        (order_hbm, order_ref),
        (density_hbm, density_ref),
        (footprint_hbm, footprint_ref),
        (cycle_hbm, cycle_ref),
    ]
    copies = [pltpu.make_async_copy(source, target, sems.at[i]) for i, (source, target) in enumerate(inputs)]
    for copy in copies:
        copy.start()
    copies[0].wait()
    first = block_start(lengths_ref)
    base, shift = split_start(first)
    after = pl.multiple_of(jnp.minimum(base + 128, deg - 128), 128)
    windows = [
        pltpu.make_async_copy(legendre_hbm.at[:, pl.ds(base, 128), :], low_ref, sems.at[6]),
        pltpu.make_async_copy(legendre_hbm.at[:, pl.ds(after, 128), :], high_ref, sems.at[7]),
    ]
    for copy in windows:
        copy.start()
    copies[1].wait()
    lane_in_block = lax.broadcasted_iota(jnp.int32, (modes, 128), 1)

    def step(k, start):
        base, shift = split_start(start)
        after = pl.multiple_of(jnp.minimum(base + 128, deg - 128), 128)
        block = jnp.where(lane_in_block >= shift, bessel_ref[:, pl.ds(base, 128)], bessel_ref[:, pl.ds(after, 128)])
        for j, row in enumerate(swap_tiles([block[16 * i : 16 * i + 16] for i in range(4)], 16)):
            block_ref[k, 16 * j : 16 * j + 16, :] = row
        return start + lengths_ref[k]

    lax.fori_loop(0, block_ref.shape[0], step, jnp.int32(0), unroll=16)
    outputs = [pltpu.make_async_copy(block_ref, send_hbm.at[:, pl.ds(16, modes), :], sems.at[8])]
    outputs[0].start()

    for copy in windows:
        copy.wait()
    slot = lax.broadcasted_iota(jnp.int32, (128, 128), 0)
    for q in range(rows_ref.shape[0]):
        rows_ref[q] = jnp.where(slot >= shift, low_ref[q], high_ref[q])
    outputs.append(pltpu.make_async_copy(rows_ref, rows_hbm, sems.at[9]))
    outputs[1].start()

    for copy in copies[2:]:
        copy.wait()
    lane = lax.broadcasted_iota(jnp.int32, (1, 128), 1)
    part = (lane >> 5) & 1
    order_slot = 2 * (lane & 31) + (lane >> 6)
    order = jnp.zeros((1, 128), jnp.int32)
    for q in range(64):
        order = jnp.where(order_slot == q, order_ref[q], order)
    sixty_four = lax.broadcasted_iota(jnp.int32, (64, 128), 0)
    pa, qa = cos_sin((sixty_four * 128 * order + 2048 * part) & 8191)
    qa = -qa
    cb, sb = cos_sin((sixty_four * 2 * order) & 8191)
    info_ref[32:33] = jnp.full((1, 128), first, jnp.int32)
    info_ref[33:34] = jnp.full((1, 128), lengths_ref[lax.axis_index("radial")], jnp.int32)
    for i in range(32):
        info_ref[i : i + 1] = jnp.where(lane < 64, order_ref[2 * i], order_ref[2 * i + 1])
    outputs.append(pltpu.make_async_copy(info_ref, info_hbm, sems.at[11]))
    outputs[2].start()
    total = jnp.zeros((2 * rows, 256), F32)
    for chunk in range(nphi // 256):
        tables = []
        for a in range(4 * chunk, 4 * chunk + 4):
            tables.append(pa[a : a + 1] * cb + qa[a : a + 1] * sb)
        table = jnp.concatenate(tables, axis=0)
        high = table.astype(BF16)
        low = (table - high.astype(F32)).astype(BF16)
        cut = slice(256 * chunk, 256 * chunk + 256)
        pixels = density_ref[0, :, cut] * footprint_ref[0, :, cut].astype(F32)
        p_high = pixels.astype(BF16)
        p_low = (pixels - p_high.astype(F32)).astype(BF16)
        total = total + jnp.dot(
            jnp.concatenate([p_high, p_low], axis=0),
            jnp.concatenate([high, low], axis=1),
            preferred_element_type=F32,
        )
    x = total[:rows, :128] + (total[:rows, 128:] + total[rows:, :128])
    row = lax.broadcasted_iota(jnp.int32, (rows, 128), 0)
    cycle = jnp.zeros((rows, 128), jnp.int32)
    for r in range(rows):
        cycle = jnp.where(row == r, cycle_ref[r], cycle)
    parity = (cycle - (NSIDE - 1)) & 1
    cos_t, sin_t = cos_sin((order * (2 - parity)) & 8191)
    other = jnp.where(part == 0, pltpu.roll(x, 96, 1), -pltpu.roll(x, 32, 1))
    four = (x * cos_t + other * sin_t).astype(BF16)
    tile_ref[...] = jnp.broadcast_to(four[None], tile_ref.shape)
    outputs.append(pltpu.make_async_copy(tile_ref, send_hbm.at[:, pl.ds(0, 16), :], sems.at[10]))
    outputs[3].start()
    for copy in outputs:
        copy.wait()


def turn_kernel(recv_ref, out_ref, wide_ref, turned_ref):
    for s in range(32):
        wide_ref[24 * s : 24 * s + 16, :] = recv_ref[s, :16].astype(F32)
    for a in range(4):
        pieces = swap_tiles([wide_ref[pl.ds(4 * a + b, 32, stride=24), :] for b in range(4)], 32)
        turned = jnp.transpose(jnp.concatenate(pieces, axis=0))
        for b in range(4):
            turned_ref[pl.ds(4 * a + b, 32, stride=24), :] = turned[32 * b : 32 * b + 32]
    for i in range(32):
        out_ref[16 * i : 16 * i + 16] = turned_ref[24 * i : 24 * i + 16, :].astype(BF16)


def block_start(lengths_ref):
    return lax.fori_loop(0, lax.axis_index("radial"), lambda k, total: total + lengths_ref[k], jnp.int32(0))


def radial_kernel(info_ref, recv_ref, out_ref, wide_ref, turned_ref):
    for s in range(32):
        wide_ref[72 * s : 72 * s + 64, :] = recv_ref[s, 16:].astype(F32)
    lane = lax.broadcasted_iota(jnp.int32, (128, 128), 1)
    row = lax.broadcasted_iota(jnp.int32, (128, 128), 0)
    slot = 32 * (row >> 5) + (lane & 31)
    keep = ((slot - info_ref[32:33]) & 127) < info_ref[33:34]

    def step(a, carry):
        x = jnp.concatenate([wide_ref[pl.ds(16 * j + a, 32, stride=72), :] for j in range(4)], axis=0)
        turned = jnp.transpose(jnp.where(keep, x, 0.0))
        for m in range(4):
            turned_ref[pl.ds(16 * m + a, 32, stride=72), :] = turned[32 * m : 32 * m + 32]
        return carry

    lax.fori_loop(0, 16, step, 0, unroll=4)
    for g in range(32):
        out_ref[g] = turned_ref[72 * g : 72 * g + 64, :].astype(BF16)


def final_kernel(info_ref, radial_ref, *refs):
    fours, rows, out_ref = refs[:8], refs[8:16], refs[16]
    four_ref, harmonic_ref, block_ref, sems = refs[17:]
    mine = lax.axis_index("shell")
    start = jnp.max(info_ref[32:33].astype(F32)).astype(jnp.int32)
    shift = info_ref[32:33] & 127
    base = info_ref[32:33] - shift
    for d in range(8):
        four_ref[:, mine ^ d] = fours[d][...].reshape(32, 16, 128)
    lane = lax.broadcasted_iota(jnp.int32, (128, 128), 1)
    slot = lax.broadcasted_iota(jnp.int32, (128, 128), 0)
    degree = base + slot + jnp.where(slot < shift, 128, 0)
    first_half = lane < 64
    for d in range(8):
        for i in range(4):
            pair = 4 * (mine ^ d) + i
            left = rows[d][2 * i : 2 * i + 2].reshape(256, 128)
            both = jnp.dot(left, four_ref[pair].reshape(128, 128), preferred_element_type=F32)
            value = jnp.where(first_half, both[:128], both[128:])
            value = jnp.where(degree >= info_ref[pl.ds(pair, 1), :], value, 0.0).astype(BF16)
            for u, packed in enumerate(swap_tiles([value[32 * j : 32 * j + 32] for j in range(4)], 32)):
                harmonic_ref[pl.ds(2 * pair + (u & 1) * 64 + (u >> 1), 32, stride=136), :] = packed.astype(F32)
    group = lax.broadcasted_iota(jnp.int32, (64, 128), 1) >> 5
    zero = jnp.zeros((64, 128), BF16)
    for g in range(32):
        right = harmonic_ref[136 * g : 136 * g + 128, :].astype(BF16)
        left = jnp.concatenate([jnp.where(group == j, radial_ref[g], zero) for j in range(4)], axis=0)
        result = lax.dot_general(left, right, (((1,), (1,)), ((), ())), preferred_element_type=F32)
        block_ref[:, g] = result.reshape(4, 64, 128).astype(BF16)
        if g % 8 == 7:
            for j in range(4):
                first = g - 7
                sem = sems.at[4 * (g // 8) + j]
                row = (32 * j + first - start) & 127

                @pl.when(row <= 120)
                def _(j=j, first=first, sem=sem, row=row):
                    pltpu.make_async_copy(block_ref.at[j, pl.ds(first, 8)], out_ref.at[pl.ds(row, 8)], sem).start()

                @pl.when(row > 120)
                def _(j=j, first=first, sem=sem, row=row):
                    for i in range(8):
                        pltpu.make_async_copy(block_ref.at[j, first + i], out_ref.at[(row + i) & 127], sem).start()

    for i in range(16):
        pltpu.make_async_copy(block_ref.at[0, pl.ds(0, 8)], out_ref.at[pl.ds(0, 8)], sems.at[i]).wait()


def on_device(density, footprint, cycle_index, order_values, block_lengths, legendre, bessel):
    shape = jax.ShapeDtypeStruct
    rows, nphi = density.shape[1:]
    deg, modes = bessel.shape[1:]
    dma = pltpu.SemaphoreType.DMA

    def swap(x, d):
        return lax.ppermute(x, "shell", [(i, i ^ d) for i in range(8)])

    send, leg_rows, info = pl.pallas_call(
        front_kernel,
        out_shape=[shape((32, 16 + modes, 128), BF16), shape((8, 128, 128), BF16), shape((40, 128), jnp.int32)],
        in_specs=[HBM_SPEC] * 7,
        out_specs=[HBM_SPEC] * 3,
        scratch_shapes=[
            pltpu.SMEM((32,), jnp.int32),
            pltpu.SMEM((rows,), jnp.int32),
            pltpu.SMEM((64,), jnp.int32),
            pltpu.VMEM((1, rows, nphi), F32),
            pltpu.VMEM((1, rows, nphi), jnp.int32),
            pltpu.VMEM((modes, deg), BF16),
            pltpu.VMEM((8, 128, 128), BF16),
            pltpu.VMEM((8, 128, 128), BF16),
            pltpu.VMEM((32, modes, 128), BF16),
            pltpu.VMEM((32, 16, 128), BF16),
            pltpu.VMEM((8, 128, 128), BF16),
            pltpu.VMEM((40, 128), jnp.int32),
            dma((12,)),
        ],
        compiler_params=params(VMEM_WHOLE),
        cost_estimate=cost(4, 1 << 21),
        name="front",
    )(block_lengths, cycle_index, order_values, density, footprint, jnp.swapaxes(bessel, 1, 2).reshape(modes, deg), legendre)
    recv = lax.all_to_all(send, "radial", split_axis=0, concat_axis=0, tiled=True)

    row_pieces = {0: leg_rows, 1: swap(leg_rows, 1)}
    for d in (4, 2, 6):
        row_pieces[d] = swap(leg_rows, d)
    for d in (4, 2, 6):
        row_pieces[d + 1] = swap(row_pieces[d], 1)

    four = pl.pallas_call(
        turn_kernel,
        out_shape=shape((512, 128), BF16),
        in_specs=[VMEM_SPEC],
        out_specs=VMEM_SPEC,
        scratch_shapes=[pltpu.VMEM((32 * 24, 128), F32)] * 2,
        compiler_params=params(),
        cost_estimate=cost(1, 1 << 19),
        name="turn",
    )(recv)

    radial = pl.pallas_call(
        radial_kernel,
        out_shape=shape((32, modes, 128), BF16),
        in_specs=[VMEM_SPEC] * 2,
        out_specs=VMEM_SPEC,
        scratch_shapes=[pltpu.VMEM((32 * 72, 128), F32)] * 2,
        compiler_params=params(),
        cost_estimate=cost(3, 1 << 20),
        name="radial_rows",
    )(info, recv)

    pieces = {0: four}
    for d in (2, 6, 4):
        pieces[d] = swap(four, d)
    own, radial = lax.optimization_barrier((four, radial))
    pieces[1] = swap(own, 1)
    for d in (2, 6, 4):
        pieces[d + 1] = swap(pieces[d], 1)

    return pl.pallas_call(
        final_kernel,
        out_shape=shape((128, modes, 128), BF16),
        in_specs=[VMEM_SPEC] * 18,
        out_specs=HBM_SPEC,
        scratch_shapes=[
            pltpu.VMEM((32, 8, 16, 128), BF16),
            pltpu.VMEM((32 * 136, 128), F32),
            pltpu.VMEM((4, 32, modes, 128), BF16),
            dma((16,)),
        ],
        compiler_params=params(),
        cost_estimate=cost(5, 1 << 22),
        name="finish",
    )(info, radial, *[pieces[d] for d in range(8)], *[row_pieces[d] for d in range(8)])


def solution(mesh):
    return jax.shard_map(
        on_device,
        mesh=mesh,
        in_specs=(
            P("radial", "shell", None),
            P("radial", "shell", None),
            P("shell"),
            P(),
            P(),
            P("shell", None, None),
            P("radial", None, "shell"),
        ),
        out_specs=P("radial", "shell", None),
        check_vma=False,
    )
```

```python
import math

import jax
import jax.numpy as jnp
from jax import lax
from jax.experimental import pallas as pl
from jax.experimental.pallas import tpu as pltpu
from jax.sharding import PartitionSpec as P

NSIDE = 1024
F32 = jnp.float32
BF16 = jnp.bfloat16
VMEM_LIMIT = 16 * 1024 * 1024
VMEM_WHOLE = 64 * 1024 * 1024

VMEM_SPEC = pl.BlockSpec(memory_space=pltpu.VMEM)
HBM_SPEC = pl.BlockSpec(memory_space=pltpu.HBM)


def params(limit=VMEM_LIMIT):
    return pltpu.CompilerParams(vmem_limit_bytes=limit)


def cost(microseconds, transferred):
    return pl.CostEstimate(flops=microseconds * 500_000_000, bytes_accessed=transferred, transcendentals=0)


def split_start(start):
    base = pl.multiple_of((start >> 7) << 7, 128)
    return base, start - base


def swap_tiles(blocks, width):
    tile = lax.broadcasted_iota(jnp.int32, (width, 128), 1) >> 5
    odd, upper = (tile & 1) == 1, tile >= 2
    middle = []
    for p in (0, 2):
        middle.append(jnp.where(odd, pltpu.roll(blocks[p + 1], 32, 1), blocks[p]))
        middle.append(jnp.where(odd, blocks[p + 1], pltpu.roll(blocks[p], 96, 1)))
    low = [jnp.where(upper, pltpu.roll(middle[p + 2], 64, 1), middle[p]) for p in (0, 1)]
    high = [jnp.where(upper, middle[p + 2], pltpu.roll(middle[p], 64, 1)) for p in (0, 1)]
    return low + high


def cos_sin(turns):
    quarter = (turns + 1024) >> 11
    x = (turns - (quarter << 11)).astype(F32) * (math.pi / 4096)
    z = x * x
    s = x + x * z * (-1.6666654611e-1 + z * (8.3321608736e-3 + z * -1.9515295891e-4))
    c = 1.0 - 0.5 * z + z * z * (4.166664568298827e-2 + z * (-1.388731625493765e-3 + z * 2.443315711809948e-5))
    odd = (quarter & 1) == 1
    even_sign = jnp.where((quarter & 2) == 2, -1.0, 1.0)
    cos = jnp.where(odd, -s, c) * even_sign
    sin = jnp.where(odd, c, s) * even_sign
    return cos, sin


def front_kernel(
    lengths_hbm, cycle_hbm, order_hbm, density_hbm, footprint_hbm, bessel_hbm, legendre_hbm, send_hbm, rows_hbm, info_hbm,
    lengths_ref, cycle_ref, order_ref, density_ref, footprint_ref, bessel_ref, low_ref, high_ref,
    block_ref, tile_ref, rows_ref, info_ref, sems,
):
    _, rows, nphi = density_ref.shape
    modes, deg = bessel_ref.shape
    inputs = [
        (lengths_hbm, lengths_ref),
        (bessel_hbm, bessel_ref),
        (order_hbm, order_ref),
        (density_hbm, density_ref),
        (footprint_hbm, footprint_ref),
        (cycle_hbm, cycle_ref),
    ]
    copies = [pltpu.make_async_copy(source, target, sems.at[i]) for i, (source, target) in enumerate(inputs)]
    for copy in copies:
        copy.start()
    copies[0].wait()
    first = block_start(lengths_ref)
    base, shift = split_start(first)
    after = pl.multiple_of(jnp.minimum(base + 128, deg - 128), 128)
    windows = [
        pltpu.make_async_copy(legendre_hbm.at[:, pl.ds(base, 128), :], low_ref, sems.at[6]),
        pltpu.make_async_copy(legendre_hbm.at[:, pl.ds(after, 128), :], high_ref, sems.at[7]),
    ]
    for copy in windows:
        copy.start()
    copies[1].wait()
    lane_in_block = lax.broadcasted_iota(jnp.int32, (modes, 128), 1)

    def step(k, start):
        base, shift = split_start(start)
        after = pl.multiple_of(jnp.minimum(base + 128, deg - 128), 128)
        block = jnp.where(lane_in_block >= shift, bessel_ref[:, pl.ds(base, 128)], bessel_ref[:, pl.ds(after, 128)])
        for j, row in enumerate(swap_tiles([block[16 * i : 16 * i + 16] for i in range(4)], 16)):
            block_ref[k, 16 * j : 16 * j + 16, :] = row
        return start + lengths_ref[k]

    lax.fori_loop(0, block_ref.shape[0], step, jnp.int32(0), unroll=16)
    outputs = [pltpu.make_async_copy(block_ref, send_hbm.at[:, pl.ds(16, modes), :], sems.at[8])]
    outputs[0].start()

    for copy in windows:
        copy.wait()
    slot = lax.broadcasted_iota(jnp.int32, (128, 128), 0)
    for q in range(rows_ref.shape[0]):
        rows_ref[q] = jnp.where(slot >= shift, low_ref[q], high_ref[q])
    outputs.append(pltpu.make_async_copy(rows_ref, rows_hbm, sems.at[9]))
    outputs[1].start()

    for copy in copies[2:]:
        copy.wait()
    lane = lax.broadcasted_iota(jnp.int32, (1, 128), 1)
    part = (lane >> 5) & 1
    order_slot = 2 * (lane & 31) + (lane >> 6)
    order = jnp.zeros((1, 128), jnp.int32)
    for q in range(64):
        order = jnp.where(order_slot == q, order_ref[q], order)
    sixty_four = lax.broadcasted_iota(jnp.int32, (64, 128), 0)
    pa, qa = cos_sin((sixty_four * 128 * order + 2048 * part) & 8191)
    qa = -qa
    cb, sb = cos_sin((sixty_four * 2 * order) & 8191)
    info_ref[32:33] = jnp.full((1, 128), first, jnp.int32)
    info_ref[33:34] = jnp.full((1, 128), lengths_ref[lax.axis_index("radial")], jnp.int32)
    for i in range(32):
        info_ref[i : i + 1] = jnp.where(lane < 64, order_ref[2 * i], order_ref[2 * i + 1])
    outputs.append(pltpu.make_async_copy(info_ref, info_hbm, sems.at[11]))
    outputs[2].start()
    total = jnp.zeros((2 * rows, 256), F32)
    for chunk in range(nphi // 256):
        tables = []
        for a in range(4 * chunk, 4 * chunk + 4):
            tables.append(pa[a : a + 1] * cb + qa[a : a + 1] * sb)
        table = jnp.concatenate(tables, axis=0)
        high = table.astype(BF16)
        low = (table - high.astype(F32)).astype(BF16)
        cut = slice(256 * chunk, 256 * chunk + 256)
        pixels = density_ref[0, :, cut] * footprint_ref[0, :, cut].astype(F32)
        p_high = pixels.astype(BF16)
        p_low = (pixels - p_high.astype(F32)).astype(BF16)
        total = total + jnp.dot(
            jnp.concatenate([p_high, p_low], axis=0),
            jnp.concatenate([high, low], axis=1),
            preferred_element_type=F32,
        )
    x = total[:rows, :128] + (total[:rows, 128:] + total[rows:, :128])
    row = lax.broadcasted_iota(jnp.int32, (rows, 128), 0)
    cycle = jnp.zeros((rows, 128), jnp.int32)
    for r in range(rows):
        cycle = jnp.where(row == r, cycle_ref[r], cycle)
    parity = (cycle - (NSIDE - 1)) & 1
    cos_t, sin_t = cos_sin((order * (2 - parity)) & 8191)
    other = jnp.where(part == 0, pltpu.roll(x, 96, 1), -pltpu.roll(x, 32, 1))
    four = (x * cos_t + other * sin_t).astype(BF16)
    tile_ref[...] = jnp.broadcast_to(four[None], tile_ref.shape)
    outputs.append(pltpu.make_async_copy(tile_ref, send_hbm.at[:, pl.ds(0, 16), :], sems.at[10]))
    outputs[3].start()
    for copy in outputs:
        copy.wait()


def turn_kernel(recv_ref, out_ref, wide_ref, turned_ref):
    for s in range(32):
        wide_ref[24 * s : 24 * s + 16, :] = recv_ref[s, :16].astype(F32)
    for a in range(4):
        pieces = swap_tiles([wide_ref[pl.ds(4 * a + b, 32, stride=24), :] for b in range(4)], 32)
        turned = jnp.transpose(jnp.concatenate(pieces, axis=0))
        for b in range(4):
            turned_ref[pl.ds(4 * a + b, 32, stride=24), :] = turned[32 * b : 32 * b + 32]
    for i in range(32):
        out_ref[16 * i : 16 * i + 16] = turned_ref[24 * i : 24 * i + 16, :].astype(BF16)


def block_start(lengths_ref):
    return lax.fori_loop(0, lax.axis_index("radial"), lambda k, total: total + lengths_ref[k], jnp.int32(0))


def radial_kernel(info_ref, recv_ref, out_ref, wide_ref, turned_ref):
    for s in range(32):
        wide_ref[72 * s : 72 * s + 64, :] = recv_ref[s, 16:].astype(F32)
    lane = lax.broadcasted_iota(jnp.int32, (128, 128), 1)
    row = lax.broadcasted_iota(jnp.int32, (128, 128), 0)
    slot = 32 * (row >> 5) + (lane & 31)
    keep = ((slot - info_ref[32:33]) & 127) < info_ref[33:34]

    def step(a, carry):
        x = jnp.concatenate([wide_ref[pl.ds(16 * j + a, 32, stride=72), :] for j in range(4)], axis=0)
        turned = jnp.transpose(jnp.where(keep, x, 0.0))
        for m in range(4):
            turned_ref[pl.ds(16 * m + a, 32, stride=72), :] = turned[32 * m : 32 * m + 32]
        return carry

    lax.fori_loop(0, 16, step, 0, unroll=4)
    for g in range(32):
        out_ref[g] = turned_ref[72 * g : 72 * g + 64, :].astype(BF16)


def final_kernel(info_ref, radial_ref, *refs):
    fours, rows, out_ref = refs[:8], refs[8:16], refs[16]
    four_ref, harmonic_ref, block_ref, sems = refs[17:]
    mine = lax.axis_index("shell")
    start = jnp.max(info_ref[32:33].astype(F32)).astype(jnp.int32)
    shift = info_ref[32:33] & 127
    base = info_ref[32:33] - shift
    for d in range(8):
        four_ref[:, mine ^ d] = fours[d][...].reshape(32, 16, 128)
    lane = lax.broadcasted_iota(jnp.int32, (128, 128), 1)
    slot = lax.broadcasted_iota(jnp.int32, (128, 128), 0)
    degree = base + slot + jnp.where(slot < shift, 128, 0)
    first_half = lane < 64
    for d in range(8):
        for i in range(4):
            pair = 4 * (mine ^ d) + i
            left = rows[d][2 * i : 2 * i + 2].reshape(256, 128)
            both = jnp.dot(left, four_ref[pair].reshape(128, 128), preferred_element_type=F32)
            value = jnp.where(first_half, both[:128], both[128:])
            value = jnp.where(degree >= info_ref[pl.ds(pair, 1), :], value, 0.0).astype(BF16)
            for u, packed in enumerate(swap_tiles([value[32 * j : 32 * j + 32] for j in range(4)], 32)):
                harmonic_ref[pl.ds(2 * pair + (u & 1) * 64 + (u >> 1), 32, stride=136), :] = packed.astype(F32)
    group = lax.broadcasted_iota(jnp.int32, (64, 128), 1) >> 5
    zero = jnp.zeros((64, 128), BF16)
    for g in range(32):
        right = harmonic_ref[136 * g : 136 * g + 128, :].astype(BF16)
        left = jnp.concatenate([jnp.where(group == j, radial_ref[g], zero) for j in range(4)], axis=0)
        result = lax.dot_general(left, right, (((1,), (1,)), ((), ())), preferred_element_type=F32)
        block_ref[:, g] = result.reshape(4, 64, 128).astype(BF16)
        if g % 4 == 3:
            for j in range(4):
                first = g - 3
                sem = sems.at[4 * (g // 4) + j]
                row = (32 * j + first - start) & 127

                @pl.when(row <= 124)
                def _(j=j, first=first, sem=sem, row=row):
                    pltpu.make_async_copy(block_ref.at[j, pl.ds(first, 4)], out_ref.at[pl.ds(row, 4)], sem).start()

                @pl.when(row > 124)
                def _(j=j, first=first, sem=sem, row=row):
                    for i in range(4):
                        pltpu.make_async_copy(block_ref.at[j, first + i], out_ref.at[(row + i) & 127], sem).start()

    for i in range(32):
        pltpu.make_async_copy(block_ref.at[0, pl.ds(0, 4)], out_ref.at[pl.ds(0, 4)], sems.at[i]).wait()


def on_device(density, footprint, cycle_index, order_values, block_lengths, legendre, bessel):
    shape = jax.ShapeDtypeStruct
    rows, nphi = density.shape[1:]
    deg, modes = bessel.shape[1:]
    dma = pltpu.SemaphoreType.DMA

    def swap(x, d):
        return lax.ppermute(x, "shell", [(i, i ^ d) for i in range(8)])

    send, leg_rows, info = pl.pallas_call(
        front_kernel,
        out_shape=[shape((32, 16 + modes, 128), BF16), shape((8, 128, 128), BF16), shape((40, 128), jnp.int32)],
        in_specs=[HBM_SPEC] * 7,
        out_specs=[HBM_SPEC] * 3,
        scratch_shapes=[
            pltpu.SMEM((32,), jnp.int32),
            pltpu.SMEM((rows,), jnp.int32),
            pltpu.SMEM((64,), jnp.int32),
            pltpu.VMEM((1, rows, nphi), F32),
            pltpu.VMEM((1, rows, nphi), jnp.int32),
            pltpu.VMEM((modes, deg), BF16),
            pltpu.VMEM((8, 128, 128), BF16),
            pltpu.VMEM((8, 128, 128), BF16),
            pltpu.VMEM((32, modes, 128), BF16),
            pltpu.VMEM((32, 16, 128), BF16),
            pltpu.VMEM((8, 128, 128), BF16),
            pltpu.VMEM((40, 128), jnp.int32),
            dma((12,)),
        ],
        compiler_params=params(VMEM_WHOLE),
        cost_estimate=cost(4, 1 << 21),
        name="front",
    )(block_lengths, cycle_index, order_values, density, footprint, jnp.swapaxes(bessel, 1, 2).reshape(modes, deg), legendre)
    recv = lax.all_to_all(send, "radial", split_axis=0, concat_axis=0, tiled=True)

    row_pieces = {0: leg_rows, 1: swap(leg_rows, 1)}
    for d in (6, 2, 4):
        row_pieces[d] = swap(leg_rows, d)
    for d in (4, 6, 2):
        row_pieces[d + 1] = swap(row_pieces[d], 1)

    four = pl.pallas_call(
        turn_kernel,
        out_shape=shape((512, 128), BF16),
        in_specs=[VMEM_SPEC],
        out_specs=VMEM_SPEC,
        scratch_shapes=[pltpu.VMEM((32 * 24, 128), F32)] * 2,
        compiler_params=params(),
        cost_estimate=cost(1, 1 << 19),
        name="turn",
    )(recv)

    radial = pl.pallas_call(
        radial_kernel,
        out_shape=shape((32, modes, 128), BF16),
        in_specs=[VMEM_SPEC] * 2,
        out_specs=VMEM_SPEC,
        scratch_shapes=[pltpu.VMEM((32 * 72, 128), F32)] * 2,
        compiler_params=params(),
        cost_estimate=cost(3, 1 << 20),
        name="radial_rows",
    )(info, recv)

    pieces = {0: four}
    for d in (6, 2, 4):
        pieces[d] = swap(four, d)
    own, radial = lax.optimization_barrier((four, radial))
    pieces[1] = swap(own, 1)
    for d in (4, 6, 2):
        pieces[d + 1] = swap(pieces[d], 1)

    return pl.pallas_call(
        final_kernel,
        out_shape=shape((128, modes, 128), BF16),
        in_specs=[VMEM_SPEC] * 18,
        out_specs=HBM_SPEC,
        scratch_shapes=[
            pltpu.VMEM((32, 8, 16, 128), BF16),
            pltpu.VMEM((32 * 136, 128), F32),
            pltpu.VMEM((4, 32, modes, 128), BF16),
            dma((32,)),
        ],
        compiler_params=params(),
        cost_estimate=cost(5, 1 << 22),
        name="finish",
    )(info, radial, *[pieces[d] for d in range(8)], *[row_pieces[d] for d in range(8)])


def solution(mesh):
    return jax.shard_map(
        on_device,
        mesh=mesh,
        in_specs=(
            P("radial", "shell", None),
            P("radial", "shell", None),
            P("shell"),
            P(),
            P(),
            P("shell", None, None),
            P("radial", None, "shell"),
        ),
        out_specs=P("radial", "shell", None),
        check_vma=False,
    )
```

```python
import math

import jax
import jax.numpy as jnp
from jax import lax
from jax.experimental import pallas as pl
from jax.experimental.pallas import tpu as pltpu
from jax.sharding import PartitionSpec as P

NSIDE = 1024
F32 = jnp.float32
BF16 = jnp.bfloat16
VMEM_LIMIT = 16 * 1024 * 1024
VMEM_WHOLE = 64 * 1024 * 1024

VMEM_SPEC = pl.BlockSpec(memory_space=pltpu.VMEM)
HBM_SPEC = pl.BlockSpec(memory_space=pltpu.HBM)


def params(limit=VMEM_LIMIT):
    return pltpu.CompilerParams(vmem_limit_bytes=limit)


def cost(microseconds, transferred):
    return pl.CostEstimate(flops=microseconds * 500_000_000, bytes_accessed=transferred, transcendentals=0)


def split_start(start):
    base = pl.multiple_of((start >> 7) << 7, 128)
    return base, start - base


def swap_tiles(blocks, width):
    tile = lax.broadcasted_iota(jnp.int32, (width, 128), 1) >> 5
    odd, upper = (tile & 1) == 1, tile >= 2
    middle = []
    for p in (0, 2):
        middle.append(jnp.where(odd, pltpu.roll(blocks[p + 1], 32, 1), blocks[p]))
        middle.append(jnp.where(odd, blocks[p + 1], pltpu.roll(blocks[p], 96, 1)))
    low = [jnp.where(upper, pltpu.roll(middle[p + 2], 64, 1), middle[p]) for p in (0, 1)]
    high = [jnp.where(upper, middle[p + 2], pltpu.roll(middle[p], 64, 1)) for p in (0, 1)]
    return low + high


def cos_sin(turns):
    quarter = (turns + 1024) >> 11
    x = (turns - (quarter << 11)).astype(F32) * (math.pi / 4096)
    z = x * x
    s = x + x * z * (-1.6666654611e-1 + z * (8.3321608736e-3 + z * -1.9515295891e-4))
    c = 1.0 - 0.5 * z + z * z * (4.166664568298827e-2 + z * (-1.388731625493765e-3 + z * 2.443315711809948e-5))
    odd = (quarter & 1) == 1
    even_sign = jnp.where((quarter & 2) == 2, -1.0, 1.0)
    cos = jnp.where(odd, -s, c) * even_sign
    sin = jnp.where(odd, c, s) * even_sign
    return cos, sin


def front_kernel(
    lengths_hbm, cycle_hbm, order_hbm, density_hbm, footprint_hbm, bessel_hbm, legendre_hbm, send_hbm, rows_hbm, info_hbm,
    lengths_ref, cycle_ref, order_ref, density_ref, footprint_ref, bessel_ref, low_ref, high_ref,
    block_ref, tile_ref, rows_ref, info_ref, sems,
):
    _, rows, nphi = density_ref.shape
    modes, deg = bessel_ref.shape
    inputs = [
        (lengths_hbm, lengths_ref),
        (bessel_hbm, bessel_ref),
        (order_hbm, order_ref),
        (density_hbm, density_ref),
        (footprint_hbm, footprint_ref),
        (cycle_hbm, cycle_ref),
    ]
    copies = [pltpu.make_async_copy(source, target, sems.at[i]) for i, (source, target) in enumerate(inputs)]
    for copy in copies:
        copy.start()
    copies[0].wait()
    first = block_start(lengths_ref)
    base, shift = split_start(first)
    after = pl.multiple_of(jnp.minimum(base + 128, deg - 128), 128)
    windows = [
        pltpu.make_async_copy(legendre_hbm.at[:, pl.ds(base, 128), :], low_ref, sems.at[6]),
        pltpu.make_async_copy(legendre_hbm.at[:, pl.ds(after, 128), :], high_ref, sems.at[7]),
    ]
    for copy in windows:
        copy.start()
    copies[1].wait()
    lane_in_block = lax.broadcasted_iota(jnp.int32, (modes, 128), 1)

    def step(k, start):
        base, shift = split_start(start)
        after = pl.multiple_of(jnp.minimum(base + 128, deg - 128), 128)
        block = jnp.where(lane_in_block >= shift, bessel_ref[:, pl.ds(base, 128)], bessel_ref[:, pl.ds(after, 128)])
        for j, row in enumerate(swap_tiles([block[16 * i : 16 * i + 16] for i in range(4)], 16)):
            block_ref[k, 16 * j : 16 * j + 16, :] = row
        return start + lengths_ref[k]

    lax.fori_loop(0, block_ref.shape[0], step, jnp.int32(0), unroll=16)
    outputs = [pltpu.make_async_copy(block_ref, send_hbm.at[:, pl.ds(16, modes), :], sems.at[8])]
    outputs[0].start()

    for copy in windows:
        copy.wait()
    slot = lax.broadcasted_iota(jnp.int32, (128, 128), 0)
    for q in range(rows_ref.shape[0]):
        rows_ref[q] = jnp.where(slot >= shift, low_ref[q], high_ref[q])
    outputs.append(pltpu.make_async_copy(rows_ref, rows_hbm, sems.at[9]))
    outputs[1].start()

    for copy in copies[2:]:
        copy.wait()
    lane = lax.broadcasted_iota(jnp.int32, (1, 128), 1)
    part = (lane >> 5) & 1
    order_slot = 2 * (lane & 31) + (lane >> 6)
    order = jnp.zeros((1, 128), jnp.int32)
    for q in range(64):
        order = jnp.where(order_slot == q, order_ref[q], order)
    sixty_four = lax.broadcasted_iota(jnp.int32, (64, 128), 0)
    pa, qa = cos_sin((sixty_four * 128 * order + 2048 * part) & 8191)
    qa = -qa
    cb, sb = cos_sin((sixty_four * 2 * order) & 8191)
    info_ref[32:33] = jnp.full((1, 128), first, jnp.int32)
    info_ref[33:34] = jnp.full((1, 128), lengths_ref[lax.axis_index("radial")], jnp.int32)
    for i in range(32):
        info_ref[i : i + 1] = jnp.where(lane < 64, order_ref[2 * i], order_ref[2 * i + 1])
    outputs.append(pltpu.make_async_copy(info_ref, info_hbm, sems.at[11]))
    outputs[2].start()
    total = jnp.zeros((2 * rows, 256), F32)
    for chunk in range(nphi // 256):
        tables = []
        for a in range(4 * chunk, 4 * chunk + 4):
            tables.append(pa[a : a + 1] * cb + qa[a : a + 1] * sb)
        table = jnp.concatenate(tables, axis=0)
        high = table.astype(BF16)
        low = (table - high.astype(F32)).astype(BF16)
        cut = slice(256 * chunk, 256 * chunk + 256)
        pixels = density_ref[0, :, cut] * footprint_ref[0, :, cut].astype(F32)
        p_high = pixels.astype(BF16)
        p_low = (pixels - p_high.astype(F32)).astype(BF16)
        total = total + jnp.dot(
            jnp.concatenate([p_high, p_low], axis=0),
            jnp.concatenate([high, low], axis=1),
            preferred_element_type=F32,
        )
    x = total[:rows, :128] + (total[:rows, 128:] + total[rows:, :128])
    row = lax.broadcasted_iota(jnp.int32, (rows, 128), 0)
    cycle = jnp.zeros((rows, 128), jnp.int32)
    for r in range(rows):
        cycle = jnp.where(row == r, cycle_ref[r], cycle)
    parity = (cycle - (NSIDE - 1)) & 1
    cos_t, sin_t = cos_sin((order * (2 - parity)) & 8191)
    other = jnp.where(part == 0, pltpu.roll(x, 96, 1), -pltpu.roll(x, 32, 1))
    four = (x * cos_t + other * sin_t).astype(BF16)
    tile_ref[...] = jnp.broadcast_to(four[None], tile_ref.shape)
    outputs.append(pltpu.make_async_copy(tile_ref, send_hbm.at[:, pl.ds(0, 16), :], sems.at[10]))
    outputs[3].start()
    for copy in outputs:
        copy.wait()


def turn_kernel(recv_ref, out_ref, wide_ref, turned_ref):
    for s in range(32):
        wide_ref[24 * s : 24 * s + 16, :] = recv_ref[s, :16].astype(F32)
    for a in range(4):
        pieces = swap_tiles([wide_ref[pl.ds(4 * a + b, 32, stride=24), :] for b in range(4)], 32)
        turned = jnp.transpose(jnp.concatenate(pieces, axis=0))
        for b in range(4):
            turned_ref[pl.ds(4 * a + b, 32, stride=24), :] = turned[32 * b : 32 * b + 32]
    for i in range(32):
        out_ref[16 * i : 16 * i + 16] = turned_ref[24 * i : 24 * i + 16, :].astype(BF16)


def block_start(lengths_ref):
    return lax.fori_loop(0, lax.axis_index("radial"), lambda k, total: total + lengths_ref[k], jnp.int32(0))


def radial_kernel(recv_ref, out_ref, wide_ref, turned_ref):
    for s in range(32):
        wide_ref[72 * s : 72 * s + 64, :] = recv_ref[s, 16:].astype(F32)
    def step(a, carry):
        x = jnp.concatenate([wide_ref[pl.ds(16 * j + a, 32, stride=72), :] for j in range(4)], axis=0)
        turned = jnp.transpose(x)
        for m in range(4):
            turned_ref[pl.ds(16 * m + a, 32, stride=72), :] = turned[32 * m : 32 * m + 32]
        return carry

    lax.fori_loop(0, 16, step, 0, unroll=4)
    for g in range(32):
        out_ref[g] = turned_ref[72 * g : 72 * g + 64, :].astype(BF16)


def final_kernel(info_ref, radial_ref, *refs):
    fours, rows, out_ref = refs[:8], refs[8:16], refs[16]
    four_ref, harmonic_ref, block_ref, sems = refs[17:]
    mine = lax.axis_index("shell")
    start = jnp.max(info_ref[32:33].astype(F32)).astype(jnp.int32)
    shift = info_ref[32:33] & 127
    base = info_ref[32:33] - shift
    for d in range(8):
        four_ref[:, mine ^ d] = fours[d][...].reshape(32, 16, 128)
    lane = lax.broadcasted_iota(jnp.int32, (128, 128), 1)
    slot = lax.broadcasted_iota(jnp.int32, (128, 128), 0)
    degree = base + slot + jnp.where(slot < shift, 128, 0)
    first_half = lane < 64
    for d in range(8):
        for i in range(4):
            pair = 4 * (mine ^ d) + i
            left = rows[d][2 * i : 2 * i + 2].reshape(256, 128)
            both = jnp.dot(left, four_ref[pair].reshape(128, 128), preferred_element_type=F32)
            value = jnp.where(first_half, both[:128], both[128:])
            value = jnp.where(degree >= info_ref[pl.ds(pair, 1), :], value, 0.0).astype(BF16)
            for u, packed in enumerate(swap_tiles([value[32 * j : 32 * j + 32] for j in range(4)], 32)):
                harmonic_ref[pl.ds(2 * pair + (u & 1) * 64 + (u >> 1), 32, stride=136), :] = packed.astype(F32)
    group = lax.broadcasted_iota(jnp.int32, (64, 128), 1) >> 5
    zero = jnp.zeros((64, 128), BF16)
    for g in range(32):
        right = harmonic_ref[136 * g : 136 * g + 128, :].astype(BF16)
        slot = 32 * group + g
        filled = jnp.where(((slot - info_ref[32:33]) & 127) < info_ref[33:34], radial_ref[g], zero)
        left = jnp.concatenate([jnp.where(group == j, filled, zero) for j in range(4)], axis=0)
        result = lax.dot_general(left, right, (((1,), (1,)), ((), ())), preferred_element_type=F32)
        block_ref[:, g] = result.reshape(4, 64, 128).astype(BF16)
        if g % 8 == 7:
            for j in range(4):
                first = g - 7
                sem = sems.at[4 * (g // 8) + j]
                row = (32 * j + first - start) & 127

                @pl.when(row <= 120)
                def _(j=j, first=first, sem=sem, row=row):
                    pltpu.make_async_copy(block_ref.at[j, pl.ds(first, 8)], out_ref.at[pl.ds(row, 8)], sem).start()

                @pl.when(row > 120)
                def _(j=j, first=first, sem=sem, row=row):
                    for i in range(8):
                        pltpu.make_async_copy(block_ref.at[j, first + i], out_ref.at[(row + i) & 127], sem).start()

    for i in range(16):
        pltpu.make_async_copy(block_ref.at[0, pl.ds(0, 8)], out_ref.at[pl.ds(0, 8)], sems.at[i]).wait()


def on_device(density, footprint, cycle_index, order_values, block_lengths, legendre, bessel):
    shape = jax.ShapeDtypeStruct
    rows, nphi = density.shape[1:]
    deg, modes = bessel.shape[1:]
    dma = pltpu.SemaphoreType.DMA

    def swap(x, d):
        return lax.ppermute(x, "shell", [(i, i ^ d) for i in range(8)])

    send, leg_rows, info = pl.pallas_call(
        front_kernel,
        out_shape=[shape((32, 16 + modes, 128), BF16), shape((8, 128, 128), BF16), shape((40, 128), jnp.int32)],
        in_specs=[HBM_SPEC] * 7,
        out_specs=[HBM_SPEC] * 3,
        scratch_shapes=[
            pltpu.SMEM((32,), jnp.int32),
            pltpu.SMEM((rows,), jnp.int32),
            pltpu.SMEM((64,), jnp.int32),
            pltpu.VMEM((1, rows, nphi), F32),
            pltpu.VMEM((1, rows, nphi), jnp.int32),
            pltpu.VMEM((modes, deg), BF16),
            pltpu.VMEM((8, 128, 128), BF16),
            pltpu.VMEM((8, 128, 128), BF16),
            pltpu.VMEM((32, modes, 128), BF16),
            pltpu.VMEM((32, 16, 128), BF16),
            pltpu.VMEM((8, 128, 128), BF16),
            pltpu.VMEM((40, 128), jnp.int32),
            dma((12,)),
        ],
        compiler_params=params(VMEM_WHOLE),
        cost_estimate=cost(4, 1 << 21),
        name="front",
    )(block_lengths, cycle_index, order_values, density, footprint, jnp.swapaxes(bessel, 1, 2).reshape(modes, deg), legendre)
    recv = lax.all_to_all(send, "radial", split_axis=0, concat_axis=0, tiled=True)

    row_pieces = {0: leg_rows, 1: swap(leg_rows, 1)}
    for d in (4, 2, 6):
        row_pieces[d] = swap(leg_rows, d)
    for d in (4, 2, 6):
        row_pieces[d + 1] = swap(row_pieces[d], 1)

    four = pl.pallas_call(
        turn_kernel,
        out_shape=shape((512, 128), BF16),
        in_specs=[VMEM_SPEC],
        out_specs=VMEM_SPEC,
        scratch_shapes=[pltpu.VMEM((32 * 24, 128), F32)] * 2,
        compiler_params=params(),
        cost_estimate=cost(1, 1 << 19),
        name="turn",
    )(recv)

    radial = pl.pallas_call(
        radial_kernel,
        out_shape=shape((32, modes, 128), BF16),
        in_specs=[VMEM_SPEC],
        out_specs=VMEM_SPEC,
        scratch_shapes=[pltpu.VMEM((32 * 72, 128), F32)] * 2,
        compiler_params=params(),
        cost_estimate=cost(3, 1 << 20),
        name="radial_rows",
    )(recv)

    pieces = {0: four}
    for d in (2, 6, 4):
        pieces[d] = swap(four, d)
    own, radial = lax.optimization_barrier((four, radial))
    pieces[1] = swap(own, 1)
    for d in (2, 6, 4):
        pieces[d + 1] = swap(pieces[d], 1)

    return pl.pallas_call(
        final_kernel,
        out_shape=shape((128, modes, 128), BF16),
        in_specs=[VMEM_SPEC] * 18,
        out_specs=HBM_SPEC,
        scratch_shapes=[
            pltpu.VMEM((32, 8, 16, 128), BF16),
            pltpu.VMEM((32 * 136, 128), F32),
            pltpu.VMEM((4, 32, modes, 128), BF16),
            dma((16,)),
        ],
        compiler_params=params(),
        cost_estimate=cost(5, 1 << 22),
        name="finish",
    )(info, radial, *[pieces[d] for d in range(8)], *[row_pieces[d] for d in range(8)])


def solution(mesh):
    return jax.shard_map(
        on_device,
        mesh=mesh,
        in_specs=(
            P("radial", "shell", None),
            P("radial", "shell", None),
            P("shell"),
            P(),
            P(),
            P("shell", None, None),
            P("radial", None, "shell"),
        ),
        out_specs=P("radial", "shell", None),
        check_vma=False,
    )
```
